256 devices in a mesh: row: 8 (over z_hi, x), col: 32 (over y, z_lo, core).
Axes of the slice: x: 4, y: 4, z: 8 (z_hi: 2, z_lo: 4; z = z_hi * 4 + z_lo), core: 2. Of those that a mesh axis runs over, the one named last changes fastest.
Arguments:
- cotangent: bfloat16 [1024, 3584, 128], P('row', 'col'), may hold values from -6 to 6
- prev_pair: bfloat16 [1024, 3584, 128], P('row', 'col'), may hold values from -12 to 12
- single_rows: bfloat16 [1024, 384], P('row'), may hold values from -6 to 6
- single_cols: bfloat16 [3584, 384], P('col'), may hold values from -6 to 6
- w_row: bfloat16 [384, 128], replicated, may hold values from -0.3125 to 0.3125
- w_col: bfloat16 [384, 128], replicated, may hold values from -0.3125 to 0.3125
- w_rec: bfloat16 [128, 128], replicated, may hold values from -0.5 to 0.5
- ln_gain: float32 [128], replicated, may hold values from 0.25 to 1.75
- ln_bias: float32 [128], replicated, may hold values from -1 to 1
- ids_rows: int32 [5, 1024], P(None, 'row'), may hold values from 0 to 1087, as said below
- ids_cols: int32 [5, 3584], P(None, 'col'), may hold values from 0 to 3647, as said below
Outputs:
- d_prev: bfloat16 [1024, 3584, 128], P('row', 'col')
- d_single_rows: float32 [1024, 384], P('row')
- d_single_cols: float32 [3584, 384], P('col')
- d_w_row: float32 [384, 128], replicated
- d_w_col: float32 [384, 128], replicated
- d_w_rec: float32 [128, 128], replicated
- d_w_rel: float32 [139, 128], replicated
- d_gain: float32 [128], replicated
- d_bias: float32 [128], replicated
The draws below stay inside these ranges and needn't reach their ends.
Inputs may be any that keep to these rules, and one draw needn't show every extreme that they name: `ids_rows`: ids rows in order: residue index, token index within its chain, chain id, entity id, symmetry id (the number of earlier chains of the same entity). Chains are contiguous; in ligand chains all tokens share one residue index; the first chain is a ligand of at least 48 tokens. The band's rows are the first 1024 column tokens, with the same ids. `ids_cols`: same layout as ids_rows; where there are more column tokens than rows, a chain begins at column token 1024.
All inputs are finite; a program needn't handle non-finite values.
Results may differ from the reference program's by a relative error of at most 0.003.
Values sent between devices are 32-bit elements; how exact they have to be, the bound alone decides.
No kernel may reach another device: no remote copies, remote signals or barrier semaphores. Data moves between devices by JAX's collectives and lax.ppermute only.
A program may use at most 64 MiB of HBM per device.

```python
import jax
import jax.numpy as jnp
from jax import lax

C = 128
S = 384
BINS = 139
ROWS = 1024
COLS = 3584


chain_span = 96


first_chain_least = 48


entity_kinds = 3


def token_ids(key):
    keys = jax.random.split(key, 5)
    position = jnp.arange(COLS, dtype=jnp.int32)
    opened = jax.random.randint(keys[0], (COLS,), 0, chain_span) == 0
    starts = opened & (position >= first_chain_least) | (position == 0) | (position == ROWS)
    chain = jnp.cumsum(starts.astype(jnp.int32)) - 1
    first = lax.cummax(jnp.where(starts, position, 0))
    within = position - first
    ligand_chain = (jax.random.randint(keys[1], (COLS,), 0, 4) == 0) | (position == 0)
    ligand_token = ligand_chain[chain]
    moving = (jax.random.randint(keys[2], (COLS,), 0, 8) != 0) & jnp.logical_not(ligand_token) & jnp.logical_not(starts)
    running = jnp.cumsum(moving.astype(jnp.int32))
    offsets = jax.random.randint(keys[3], (COLS,), 0, 64)
    climbed = running - running[first]
    offsets = offsets.at[chain[ROWS - 1]].set(ROWS + 63 - climbed[ROWS - 1])
    offsets = offsets.at[chain[COLS - 1]].set(COLS + 63 - climbed[COLS - 1])
    residue = climbed + offsets[chain]
    entity = jax.random.randint(keys[4], (COLS,), 0, entity_kinds)[chain]
    kinds = jnp.arange(entity_kinds, dtype=jnp.int32)
    matches = entity[:, None] == kinds[None, :]
    copies = jnp.cumsum((starts[:, None] & matches).astype(jnp.int32), axis=0)
    symmetry = jnp.sum(jnp.where(matches, copies, 0), axis=1) - 1
    return jnp.stack([residue, within, chain, entity, symmetry]).astype(jnp.int32)


def draw_ids_rows(key, part):
    return token_ids(key)[:, :ROWS]


def draw_ids_cols(key, part):
    return token_ids(key)


def level_of(key, shape, cuts, smallest, high):
    level, own = 1.0, jax.random.fold_in(key, 6)
    for dim, blocks in cuts:
        draws = jnp.exp(jax.random.uniform(jax.random.fold_in(own, dim), (blocks,), jnp.float32, smallest / len(cuts), high / len(cuts)))
        level = level * jnp.repeat(draws, shape[dim] // blocks).reshape([-1 if axis == dim else 1 for axis in range(len(shape))])
    return level


def scatter_about(own_key, shape, deviation, limit, shards=(), kind=jnp.bfloat16):
    array = jax.random.normal(own_key, shape, jnp.float32) * deviation
    if len(shards) > 0:
        array = level_of(own_key, shape, shards, -0.22, 0.18) * array
    return jnp.clip(array, min=-limit, max=limit).astype(kind)


def setup_inputs(seed: int = 0) -> dict:
    seeds = jax.random.split(jax.random.key(seed), 12)
    cotangent = scatter_about(seeds[0], (ROWS, COLS, C), 1.0, 6.0, ((0, 8), (1, 32)))
    prev_pair = scatter_about(seeds[1], (ROWS, COLS, C), 2.0, 12.0, ((0, 8), (1, 32)))
    single_rows = scatter_about(seeds[2], (ROWS, S), 1.0, 6.0, ((0, 8),))
    single_cols = scatter_about(seeds[3], (COLS, S), 1.0, 6.0, ((0, 32),))
    w_row = scatter_about(seeds[4], (S, C), S ** -0.5, 0.3125)
    w_col = scatter_about(seeds[5], (S, C), S ** -0.5, 0.3125)
    w_rec = scatter_about(seeds[6], (C, C), C ** -0.5, 0.5)
    ln_gain = jnp.clip(1.0 + 0.15 * jax.random.normal(seeds[7], (C,), jnp.float32), 0.25, 1.75)
    ln_bias = jnp.clip(jax.random.uniform(seeds[8], (C,), jnp.float32, -1.0, 1.0), -1.0, 1.0)
    ids_rows = draw_ids_rows(jax.random.fold_in(seeds[11], 71), 0)
    ids_cols = draw_ids_cols(jax.random.fold_in(seeds[11], 71), 0)
    return dict(cotangent=cotangent, prev_pair=prev_pair, single_rows=single_rows, single_cols=single_cols, w_row=w_row, w_col=w_col, w_rec=w_rec, ln_gain=ln_gain, ln_bias=ln_bias, ids_rows=ids_rows, ids_cols=ids_cols)


block_rows = 8

def layer_terms(cot, prev, norm_gain, norm_bias, w_rec):
    width = cot.shape[-1]
    flat_cot = cot.reshape(-1, width)
    x = prev.reshape(-1, width).astype(jnp.float32)
    input_mean = lax.optimization_barrier(jnp.mean(x, axis=1, keepdims=True))
    centered_input = x - input_mean
    inverse_deviation = lax.rsqrt(lax.optimization_barrier(jnp.mean(centered_input * centered_input, axis=1, keepdims=True)) + 1e-05)
    standardized_input = centered_input * inverse_deviation
    normalized_input = (standardized_input * norm_gain + norm_bias).astype(jnp.bfloat16)
    rec_grad = lax.dot_general(normalized_input, flat_cot, (((0,), (0,)), ((), ())), preferred_element_type=jnp.float32)
    output_gradient = lax.dot_general(flat_cot, w_rec, (((1,), (1,)), ((), ())), preferred_element_type=jnp.float32)
    norm_gain_gradient = lax.optimization_barrier(jnp.sum(output_gradient * standardized_input, axis=0))
    bias_grad = lax.optimization_barrier(jnp.sum(output_gradient, axis=0))
    scaled_gradient = output_gradient * norm_gain
    backward_result = inverse_deviation * (scaled_gradient - lax.optimization_barrier(jnp.mean(scaled_gradient, axis=1, keepdims=True)) - standardized_input * lax.optimization_barrier(jnp.mean(scaled_gradient * standardized_input, axis=1, keepdims=True)))
    return (backward_result.astype(jnp.bfloat16).reshape(cot.shape), rec_grad, norm_gain_gradient, bias_grad)

def relpos_bins(ids_i, ids_j):
    same_chain = ids_i[2][:, None] == ids_j[2][None, :]
    same_res = same_chain & (ids_i[0][:, None] == ids_j[0][None, :])
    same_entity = ids_i[3][:, None] == ids_j[3][None, :]
    res_bin = jnp.where(same_chain, jnp.clip(ids_i[0][:, None] - ids_j[0][None, :] + 32, 0, 64), 65)
    tok_bin = jnp.where(same_res, jnp.clip(ids_i[1][:, None] - ids_j[1][None, :] + 32, 0, 64), 65)
    chain_bin = jnp.where(same_entity & jnp.logical_not(same_chain), jnp.clip(ids_i[4][:, None] - ids_j[4][None, :] + 2, 0, 4), 5)
    return (res_bin.reshape(-1).astype(jnp.int32), tok_bin.reshape(-1).astype(jnp.int32), same_entity.reshape(-1), chain_bin.reshape(-1).astype(jnp.int32))

def relpos_grad(ids_i, ids_j, flat_cot):
    res_bin, tok_bin, same_entity, chain_bin = relpos_bins(ids_i, ids_j)
    wide = flat_cot.astype(jnp.float32)
    parts = [jax.ops.segment_sum(wide, res_bin, num_segments=66), jax.ops.segment_sum(wide, tok_bin, num_segments=66), lax.optimization_barrier(jnp.sum(jnp.where(same_entity[:, None], wide, 0.0), axis=0, keepdims=True)), jax.ops.segment_sum(wide, chain_bin, num_segments=6)]
    return jnp.concatenate(parts, axis=0)

def reference(cotangent, prev_pair, single_rows, single_cols, w_row, w_col, w_rec, ln_gain, ln_bias, ids_rows, ids_cols):
    width = cotangent.shape[-1]
    blocks = ROWS // block_rows
    cot_blocks = cotangent.reshape(blocks, block_rows, COLS, width)
    prev_blocks = prev_pair.reshape(blocks, block_rows, COLS, width)
    id_blocks = jnp.transpose(ids_rows.reshape(5, blocks, block_rows), (1, 0, 2))

    def step(carry, item):
        cot, prev, ids_i = item
        backward_result, rec_grad, norm_gain_gradient, bias_grad = layer_terms(cot, prev, ln_gain, ln_bias, w_rec)
        rel_grad = relpos_grad(ids_i, ids_cols, cot.reshape(-1, width))
        row_part = lax.optimization_barrier(jnp.sum(cot, axis=1, dtype=jnp.float32))
        col_part = lax.optimization_barrier(jnp.sum(cot, axis=0, dtype=jnp.float32))
        totals = (carry[0] + rec_grad, carry[1] + norm_gain_gradient, carry[2] + bias_grad, carry[3] + rel_grad, carry[4] + col_part)
        return (totals, (backward_result, row_part))
    init = (jnp.zeros((width, width), jnp.float32), jnp.zeros((width,), jnp.float32), jnp.zeros((width,), jnp.float32), jnp.zeros((BINS, width), jnp.float32), jnp.zeros((COLS, width), jnp.float32))
    totals, (backward_result, row_sum) = lax.scan(step, init, (cot_blocks, prev_blocks, id_blocks))
    rec_grad, norm_gain_gradient, bias_grad, rel_grad, col_sum = totals
    row_sum = row_sum.reshape(ROWS, width)
    high = lax.Precision.HIGHEST
    d_single_rows = jnp.dot(row_sum, w_row.astype(jnp.float32).T, precision=high)
    d_single_cols = jnp.dot(col_sum, w_col.astype(jnp.float32).T, precision=high)
    d_w_row = jnp.dot(single_rows.astype(jnp.float32).T, row_sum, precision=high)
    d_w_col = jnp.dot(single_cols.astype(jnp.float32).T, col_sum, precision=high)
    return (backward_result.reshape(ROWS, COLS, width), d_single_rows, d_single_cols, d_w_row, d_w_col, rec_grad, rel_grad, norm_gain_gradient, bias_grad)
```

```python
import functools

import jax
import jax.numpy as jnp
from jax import lax
from jax.experimental import pallas as pl
from jax.experimental.pallas import tpu as pltpu
from jax.sharding import Mesh, PartitionSpec as P

F32, BF16 = jnp.float32, jnp.bfloat16
C = 128
S = 384
BINS = 139
SUB = 8
CHUNK = 40
PARTS = 32
ROW = ("zh", "x")
COLG = ("y", "zl")


def dot(a, b, dims):
    return lax.dot_general(a, b, (dims, ((), ())), preferred_element_type=F32)


def split_dot(a, b, dims, split_left):
    x = a if split_left else b
    hi = x.astype(BF16)
    rest = x - hi.astype(F32)
    mid = rest.astype(BF16)
    low = (rest - mid.astype(F32)).astype(BF16)
    if split_left:
        return dot(hi, b, dims) + (dot(mid, b, dims) + dot(low, b, dims))
    return dot(a, hi, dims) + (dot(a, mid, dims) + dot(a, low, dims))


def standardize(prev):
    ones = jnp.full((C, C), 1.0 / C, BF16)
    mean = dot(prev, ones, ((1,), (0,)))
    centered = prev.astype(F32) - mean
    var = dot((centered * centered).astype(BF16), ones, ((1,), (0,)))
    rstd = lax.rsqrt(var + 1e-05)
    return centered * rstd, rstd


def reduce_kernel(cols, steps, rows, core_ref, cot_ref, prev_ref, idr_ref, idc_ref, sr_ref, sc_ref,
                  send_ref, keep_ref, colp_ref, acc, rowp, colp, buf):
    step = pl.program_id(0)

    @pl.when(step == 0)
    def _():
        acc[...] = jnp.zeros_like(acc)
        colp[...] = jnp.zeros_like(colp)

    n = SUB * cols
    idr = idr_ref[...].astype(F32)
    idc = idc_ref[...].astype(F32)
    lane = lax.broadcasted_iota(jnp.int32, (SUB, idr.shape[1]), 1)
    sub = lax.broadcasted_iota(jnp.int32, (SUB, idr.shape[1]), 0)
    flat_lane = lax.broadcasted_iota(jnp.int32, (16, n), 1)
    flat_sub = lax.broadcasted_iota(jnp.int32, (16, n), 0)
    rowind = jnp.where((flat_lane >= flat_sub * cols) & (flat_lane < (flat_sub + 1) * cols), 1.0, 0.0).astype(BF16)

    for b in range(rows // SUB):
        first = step * rows + b * SUB
        cot = cot_ref[b * SUB:(b + 1) * SUB].reshape(n, C)
        prev = prev_ref[b * SUB:(b + 1) * SUB].reshape(n, C)
        xhat, _ = standardize(prev)
        mask = lane == sub + first
        di = [jnp.sum(jnp.where(mask, idr[k:k + 1], 0.0), axis=1, keepdims=True) for k in range(5)]
        dj = [idc[k:k + 1] for k in range(5)]
        same_chain = di[2] == dj[2]
        same_res = same_chain & (di[0] == dj[0])
        same_entity = di[3] == dj[3]
        r = jnp.where(same_chain, jnp.clip(di[0] - dj[0] + 32.0, 0.0, 64.0), 65.0)
        t = jnp.where(same_res, jnp.clip(di[1] - dj[1] + 32.0, 0.0, 64.0), 65.0) + 66.0
        e = jnp.where(same_entity, 132.0, -1.0)
        c = jnp.where(same_entity & jnp.logical_not(same_chain), jnp.clip(di[4] - dj[4] + 2.0, 0.0, 4.0), 5.0) + 133.0
        r, t, e, c = [
            jnp.concatenate([v[s:s + 1] for s in range(SUB)], axis=1) for v in (r, t, e, c)
        ]

        def hot(lo, hi, *codes):
            q = lax.broadcasted_iota(jnp.int32, (hi - lo, n), 0).astype(F32) + float(lo)
            hit = q == codes[0]
            for code in codes[1:]:
                hit = hit | (q == code)
            return jnp.where(hit, 1.0, 0.0).astype(BF16)

        left = jnp.concatenate(
            [
                jnp.transpose(xhat.astype(BF16)),
                hot(0, 64, r), hot(64, 80, r, t), hot(80, 128, t), hot(128, 144, t, e, c),
                rowind,
            ],
            axis=0,
        )
        out = dot(left, cot, ((1,), (0,)))
        acc[...] += out[:272]
        rowp[pl.ds(pl.multiple_of(first, SUB), SUB), :] = out[272:280]
        wide = cot_ref[b * SUB].astype(F32)
        for s in range(1, SUB):
            wide += cot_ref[b * SUB + s].astype(F32)
        colp[...] += wide

    @pl.when(step == steps - 1)
    def _():
        dwr = split_dot(sr_ref[...], rowp[...], ((0,), (0,)), False)
        dwc = split_dot(sc_ref[...], colp[...], ((0,), (0,)), False)
        total = acc[...]
        colp_ref[...] = colp[...]
        for k in range(PARTS):
            half, place = k // 16, k % 16
            buf[half, place, 0:4] = total[4 * k:4 * k + 4]
            buf[half, place, 4:8] = rowp[4 * k:4 * k + 4]
            lo, hi = 128 + 5 * k, min(128 + 5 * k + 5, 272)
            if lo < hi:
                buf[half, place, 8:8 + hi - lo] = total[lo:hi]
            pad = 8 + max(hi - lo, 0)
            buf[half, place, pad:16] = jnp.zeros((16 - pad, C), F32)
            buf[half, place, 16:28] = dwr[12 * k:12 * k + 12]
            buf[half, place, 28:40] = dwc[12 * k:12 * k + 12]
        core = core_ref[0]
        keep_ref[...] = buf[core]
        send_ref[...] = buf[1 - core]


def local_reductions(core, cot, prev, idr, idc, sr, sc):
    rows, cols = cot.shape[:2]
    per = 16
    steps = rows // per
    whole = lambda a: pl.BlockSpec(a.shape, lambda i: (0,) * a.ndim)
    part = jax.ShapeDtypeStruct((16, CHUNK, C), F32)
    colo = jax.ShapeDtypeStruct((cols, C), F32)
    return pl.pallas_call(
        functools.partial(reduce_kernel, cols, steps, per),
        grid=(steps,),
        in_specs=[
            pl.BlockSpec(memory_space=pltpu.SMEM),
            pl.BlockSpec((per, cols, C), lambda i: (i, 0, 0)),
            pl.BlockSpec((per, cols, C), lambda i: (i, 0, 0)),
            whole(idr), whole(idc), whole(sr), whole(sc),
        ],
        out_specs=[whole(part), whole(part), whole(colo)],
        out_shape=[part, part, colo],
        scratch_shapes=[
            pltpu.VMEM((272, C), F32),
            pltpu.VMEM((rows, C), F32),
            pltpu.VMEM((cols, C), F32),
            pltpu.VMEM((2, 16, CHUNK, C), F32),
        ],
        compiler_params=pltpu.CompilerParams(vmem_limit_bytes=48 * 1024 * 1024),
        name="local_reductions",
    )(core, cot, prev, idr, idc, sr, sc)


def prev_kernel(cols, rows, cot_ref, prev_ref, w_ref, gain_ref, *rest):
    out_ref = rest[-1]
    n = SUB * cols
    gain = gain_ref[...]
    w = w_ref[...]
    gain_mean = jnp.sum(w.astype(F32) * jnp.transpose(jnp.broadcast_to(gain, (C, C))), axis=0, keepdims=True) * (1.0 / C)
    mean_w = jnp.broadcast_to(gain_mean, (C, C)).astype(BF16)
    both = jnp.concatenate([w, mean_w], axis=0)
    ones = jnp.full((C, C), 1.0 / C, BF16)
    for b in range(rows // SUB):
        cot = cot_ref[b * SUB:(b + 1) * SUB].reshape(n, C)
        prev = prev_ref[b * SUB:(b + 1) * SUB].reshape(n, C)
        xhat, rstd = standardize(prev)
        y = dot(cot, both, ((1,), (1,)))
        g = y[:, :C] * gain
        corr = dot((g * xhat).astype(BF16), ones, ((1,), (0,)))
        res = rstd * (g - y[:, C:] - xhat * corr)
        out_ref[b * SUB:(b + 1) * SUB] = res.astype(BF16).reshape(SUB, cols, C)


def prev_grad(lo, hi, per, cot, prev, w, gain, into):
    rows, cols = cot.shape[:2]
    block = pl.BlockSpec((per, cols, C), lambda i: (lo // per + i, 0, 0))
    args = [cot, prev, w, gain]
    specs = [block, block, pl.BlockSpec((C, C), lambda i: (0, 0)), pl.BlockSpec((1, C), lambda i: (0, 0))]
    if into is not None:
        args.append(into)
        specs.append(pl.BlockSpec(memory_space=pl.ANY))
    pairs = (hi - lo) * cols
    return pl.pallas_call(
        functools.partial(prev_kernel, cols, per),
        grid=((hi - lo) // per,),
        in_specs=specs,
        out_specs=block,
        out_shape=jax.ShapeDtypeStruct(cot.shape, BF16),
        input_output_aliases={4: 0} if into is not None else {},
        compiler_params=pltpu.CompilerParams(vmem_limit_bytes=48 * 1024 * 1024),
        cost_estimate=pl.CostEstimate(flops=pairs * C * C * 10, bytes_accessed=pairs * C * 6, transcendentals=0),
        name="prev_grad",
    )(*args)


def final_kernel(core_ref, own_ref, other_ref, cols_ref, wr_ref, wc_ref, w_ref, gain_ref, bias_ref,
                 dsr_ref, dsc_ref, dwr_ref, dwc_ref, rec_ref, rel_ref, dg_ref, db_ref, buf, m, rows, rel):
    core = core_ref[0]
    buf[core] = own_ref[...]
    buf[1 - core] = other_ref[...]
    for k in range(PARTS):
        half, place = k // 16, k % 16
        m[4 * k:4 * k + 4] = buf[half, place, 0:4]
        rows[4 * k:4 * k + 4] = buf[half, place, 4:8]
        lo, hi = 5 * k, min(5 * k + 5, 144)
        if lo < hi:
            rel[lo:hi] = buf[half, place, 8:8 + hi - lo]
        dwr_ref[12 * k:12 * k + 12] = buf[half, place, 16:28]
        dwc_ref[12 * k:12 * k + 12] = buf[half, place, 28:40]
    rel_ref[...] = rel[0:BINS]
    total = jnp.sum(rel[133:139], axis=0, keepdims=True)
    big = m[...]
    w = w_ref[...].astype(F32)
    gain_col = jnp.transpose(jnp.broadcast_to(gain_ref[...], (C, C)))
    bias_col = jnp.transpose(jnp.broadcast_to(bias_ref[...], (C, C)))
    rec_ref[...] = gain_col * big + bias_col * total
    dg_ref[...] = jnp.sum(jnp.transpose(w * big), axis=0, keepdims=True)
    db_ref[...] = jnp.sum(jnp.transpose(w * total), axis=0, keepdims=True)
    dsr_ref[...] = split_dot(rows[...], wr_ref[...], ((1,), (1,)), True)
    dsc_ref[...] = split_dot(cols_ref[...], wc_ref[...], ((1,), (1,)), True)


def finish(core, own, other, cols, wr, wc, w, gain, bias, nrows):
    f = lambda *s: jax.ShapeDtypeStruct(s, F32)
    vmem = pl.BlockSpec(memory_space=pltpu.VMEM)
    return pl.pallas_call(
        final_kernel,
        in_specs=[pl.BlockSpec(memory_space=pltpu.SMEM)] + [vmem] * 8,
        out_specs=[vmem] * 8,
        out_shape=[f(nrows, S), f(cols.shape[0], S), f(S, C), f(S, C), f(C, C), f(BINS, C), f(1, C), f(1, C)],
        scratch_shapes=[
            pltpu.VMEM((2, 16, CHUNK, C), F32),
            pltpu.VMEM((C, C), F32),
            pltpu.VMEM((nrows, C), F32),
            pltpu.VMEM((144, C), F32),
        ],
        compiler_params=pltpu.CompilerParams(vmem_limit_bytes=48 * 1024 * 1024),
        name="finish",
    )(core, own, other, cols, wr, wc, w, gain, bias)


def swap(a, axis, size, bit):
    return lax.ppermute(a, axis, [(i, i ^ bit) for i in range(size)])


def shards(cot, prev, single_rows, single_cols, w_row, w_col, w_rec, gain, bias, ids_rows, ids_cols):
    core = lax.axis_index("c").astype(jnp.int32).reshape(1)
    gain2, bias2 = gain.reshape(1, C), bias.reshape(1, C)
    send, keep, col_part = local_reductions(core, cot, prev, ids_rows, ids_cols, single_rows, single_cols)
    half = keep + swap(send, "c", 2, 1)
    chunks = lax.all_to_all(half, COLG, 0, 0)
    mine = jnp.sum(chunks, axis=0)
    z = jnp.concatenate([mine, col_part], axis=0)
    d_prev = None
    cuts = (0, 32, 80, 128)
    for turn, (axis, size, bit) in enumerate((("x", 4, 1), ("x", 4, 3), ("zh", 2, 1))):
        got = swap(z, axis, size, bit)
        if d_prev is None:
            c2, p2, z = lax.optimization_barrier((cot, prev, z))
        else:
            d_prev, z = lax.optimization_barrier((d_prev, z))
        d_prev = prev_grad(cuts[turn], cuts[turn + 1], 16, c2, p2, w_rec, gain2, d_prev)
        z = z + got
    kept = lax.broadcasted_iota(jnp.int32, (CHUNK, 1), 0) // 4 == 1
    full = jnp.where(kept, mine, z[:CHUNK])
    col_sum = z[CHUNK:]
    own = lax.all_to_all(jnp.broadcast_to(full[None], (16, CHUNK, C)), COLG, 0, 0)
    other = swap(own, "c", 2, 1)
    dsr, dsc, dwr, dwc, rec, rel, dg, db = finish(
        core, own, other, col_sum, w_row, w_col, w_rec, gain2, bias2, cot.shape[0]
    )
    return d_prev, dsr, dsc, dwr, dwc, rec, rel, dg.reshape(C), db.reshape(C)


def solution(mesh):
    fine = Mesh(mesh.devices.reshape(2, 4, 4, 4, 2), ("zh", "x", "y", "zl", "c"))
    row, col = ROW, COLG + ("c",)
    return jax.shard_map(
        shards,
        mesh=fine,
        in_specs=(
            P(row, col, None), P(row, col, None), P(row, None), P(col, None),
            P(), P(), P(), P(), P(), P(None, row), P(None, col),
        ),
        out_specs=(P(row, col, None), P(row, None), P(col, None), P(), P(), P(), P(), P(), P()),
        check_vma=False,
    )
```

```python
import functools

import jax
import jax.numpy as jnp
from jax import lax
from jax.experimental import pallas as pl
from jax.experimental.pallas import tpu as pltpu
from jax.sharding import Mesh, PartitionSpec as P

F32, BF16 = jnp.float32, jnp.bfloat16
C = 128
S = 384
BINS = 139
SUB = 16
CHUNK = 40
PARTS = 32
VMEM = 60 * 1024 * 1024
ROW = ("zh", "x")
COLG = ("y", "zl")


def dot(a, b, dims):
    return lax.dot_general(a, b, (dims, ((), ())), preferred_element_type=F32)


def split_dot(a, b, dims, split_left):
    x = a if split_left else b
    hi = x.astype(BF16)
    rest = x - hi.astype(F32)
    mid = rest.astype(BF16)
    low = (rest - mid.astype(F32)).astype(BF16)
    if split_left:
        return dot(hi, b, dims) + (dot(mid, b, dims) + dot(low, b, dims))
    return dot(a, hi, dims) + (dot(a, mid, dims) + dot(a, low, dims))


def reduce_kernel(cols, steps, rows, core_ref, cot_ref, prev_ref, w_ref, gain_ref, bias_ref, idr_ref, idc_ref, sr_hbm, sc_hbm,
                  send_ref, keep_ref, colp_ref, dprev_ref, acc, gains, gcol, bcol, rowp, colp, buf, sr_ref, sc_ref, sems):
    step = pl.program_id(0)
    fetch = [pltpu.make_async_copy(sr_hbm, sr_ref, sems.at[0]), pltpu.make_async_copy(sc_hbm, sc_ref, sems.at[1])]

    @pl.when(step == 0)
    def _():
        acc[...] = jnp.zeros_like(acc)
        gains[...] = jnp.zeros_like(gains)
        gcol[...] = jnp.transpose(jnp.broadcast_to(gain_ref[...], (C, C)))
        bcol[...] = jnp.transpose(jnp.broadcast_to(bias_ref[...], (C, C)))
        colp[...] = jnp.zeros_like(colp)
        for f in fetch:
            f.start()

    n = SUB * cols
    idr = idr_ref[...].astype(F32)
    idc = idc_ref[...].astype(F32)
    gain, bias = gcol[:, 0:1], bcol[:, 0:1]
    lane = lax.broadcasted_iota(jnp.int32, (SUB, idr.shape[1]), 1)
    sub = lax.broadcasted_iota(jnp.int32, (SUB, idr.shape[1]), 0)
    flat_lane = lax.broadcasted_iota(jnp.int32, (16, n), 1)
    flat_sub = lax.broadcasted_iota(jnp.int32, (16, n), 0)
    rowind = jnp.where((flat_lane >= flat_sub * cols) & (flat_lane < (flat_sub + 1) * cols), 1.0, 0.0).astype(BF16)

    def mean(a):
        return jnp.sum(a, axis=0, keepdims=True) * (1.0 / C)

    for b in range(0, rows, SUB):
        first = step * rows + b
        cot = cot_ref[b:b + SUB].reshape(n, C)
        x = jnp.transpose(prev_ref[b:b + SUB].reshape(n, C)).astype(F32)
        centered = x - mean(x)
        rstd = lax.rsqrt(mean(centered * centered) + 1e-05)
        xhat = centered * rstd
        normed = (xhat * gain + bias).astype(BF16)
        g = dot(w_ref[...], cot, ((1,), (1,))) * gain
        gx = g * xhat
        share = gx[:, 0:C]
        for lo in range(C, n, C):
            share += gx[:, lo:lo + C]
        gains[...] += share
        res = (rstd * (g - mean(g) - xhat * mean(gx))).astype(BF16)
        dprev_ref[b:b + SUB] = jnp.transpose(res).reshape(SUB, cols, C)
        mask = lane == sub + first
        di = [jnp.sum(jnp.where(mask, idr[k:k + 1], 0.0), axis=1, keepdims=True) for k in range(5)]
        dj = [idc[k:k + 1] for k in range(5)]
        same_chain = di[2] == dj[2]
        same_res = same_chain & (di[0] == dj[0])
        same_entity = di[3] == dj[3]
        r = jnp.where(same_chain, jnp.clip(di[0] - dj[0] + 32.0, 0.0, 64.0), 65.0)
        t = jnp.where(same_res, jnp.clip(di[1] - dj[1] + 32.0, 0.0, 64.0), 65.0) + 66.0
        e = jnp.where(same_entity, 132.0, -1.0)
        c = jnp.where(same_entity & jnp.logical_not(same_chain), jnp.clip(di[4] - dj[4] + 2.0, 0.0, 4.0), 5.0) + 133.0
        r, t, e, c = [jnp.concatenate([v[s:s + 1] for s in range(SUB)], axis=1) for v in (r, t, e, c)]

        def hot(lo, hi, *codes):
            q = lax.broadcasted_iota(jnp.int32, (hi - lo, n), 0).astype(F32) + float(lo)
            hit = q == codes[0]
            for code in codes[1:]:
                hit = hit | (q == code)
            return jnp.where(hit, 1.0, 0.0).astype(BF16)

        left = jnp.concatenate(
            [normed, hot(0, 64, r), hot(64, 80, r, t), hot(80, 128, t), hot(128, 144, t, e, c), rowind], axis=0
        )
        out = dot(left, cot, ((1,), (0,)))
        acc[...] += out[:272]
        rowp[pl.ds(pl.multiple_of(first, SUB), SUB), :] = out[272:288]
        wide = cot_ref[b].astype(F32)
        for s in range(1, SUB):
            wide += cot_ref[b + s].astype(F32)
        colp[...] += wide

    @pl.when(step == steps - 1)
    def _():
        for f in fetch:
            f.wait()
        dwr = split_dot(sr_ref[...], rowp[...], ((0,), (0,)), False)
        dwc = split_dot(sc_ref[...], colp[...], ((0,), (0,)), False)
        acc[267:268] = jnp.sum(jnp.transpose(gains[...]), axis=0, keepdims=True) / gain_ref[...]
        total = acc[...]
        colp_ref[...] = colp[...]
        for k in range(PARTS):
            half, place = k // 16, k % 16
            buf[half, place, 0:4] = total[4 * k:4 * k + 4]
            buf[half, place, 4:8] = rowp[4 * k:4 * k + 4]
            lo, hi = 128 + 5 * k, min(128 + 5 * k + 5, 272)
            if lo < hi:
                buf[half, place, 8:8 + hi - lo] = total[lo:hi]
            pad = 8 + max(hi - lo, 0)
            buf[half, place, pad:16] = jnp.zeros((16 - pad, C), F32)
            buf[half, place, 16:28] = dwr[12 * k:12 * k + 12]
            buf[half, place, 28:40] = dwc[12 * k:12 * k + 12]
        core = core_ref[0]
        keep_ref[...] = buf[core]
        send_ref[...] = buf[1 - core]


def local_reductions(core, cot, prev, w, gain, bias, idr, idc, sr, sc, per=32):
    rows, cols = cot.shape[:2]
    steps = rows // per
    whole = lambda a: pl.BlockSpec(a.shape, lambda i: (0,) * a.ndim)
    block = pl.BlockSpec((per, cols, C), lambda i: (i, 0, 0))
    part = jax.ShapeDtypeStruct((16, CHUNK, C), F32)
    colo = jax.ShapeDtypeStruct((cols, C), F32)
    return pl.pallas_call(
        functools.partial(reduce_kernel, cols, steps, per),
        grid=(steps,),
        in_specs=[
            pl.BlockSpec(memory_space=pltpu.SMEM),
            block, block,
            whole(w), whole(gain), whole(bias), whole(idr), whole(idc),
            pl.BlockSpec(memory_space=pltpu.HBM), pl.BlockSpec(memory_space=pltpu.HBM),
        ],
        out_specs=[pl.BlockSpec(memory_space=pltpu.VMEM)] * 3 + [block],
        out_shape=[part, part, colo] + [jax.ShapeDtypeStruct(cot.shape, BF16)],
        scratch_shapes=[
            pltpu.VMEM((272, C), F32),
            pltpu.VMEM((C, C), F32),
            pltpu.VMEM((C, C), F32),
            pltpu.VMEM((C, C), F32),
            pltpu.VMEM((rows, C), F32),
            pltpu.VMEM((cols, C), F32),
            pltpu.VMEM((2, 16, CHUNK, C), F32),
            pltpu.VMEM(sr.shape, BF16),
            pltpu.VMEM(sc.shape, BF16),
            pltpu.SemaphoreType.DMA((2,)),
        ],
        compiler_params=pltpu.CompilerParams(vmem_limit_bytes=VMEM),
        name="local_reductions",
    )(core, cot, prev, w, gain, bias, idr, idc, sr, sc)


def final_kernel(core_ref, own_ref, other_ref, cols_ref, wr_ref, wc_ref, w_ref,
                 dsr_ref, dsc_ref, dwr_ref, dwc_ref, rec_ref, rel_ref, dg_ref, db_ref, buf, m, rows, rel):
    core = core_ref[0]
    buf[core] = own_ref[...]
    buf[1 - core] = other_ref[...]
    for k in range(PARTS):
        half, place = k // 16, k % 16
        m[4 * k:4 * k + 4] = buf[half, place, 0:4]
        rows[4 * k:4 * k + 4] = buf[half, place, 4:8]
        lo, hi = 5 * k, min(5 * k + 5, 144)
        if lo < hi:
            rel[lo:hi] = buf[half, place, 8:8 + hi - lo]
        dwr_ref[12 * k:12 * k + 12] = buf[half, place, 16:28]
        dwc_ref[12 * k:12 * k + 12] = buf[half, place, 28:40]
    rel_ref[...] = rel[0:BINS]
    total = jnp.sum(rel[133:139], axis=0, keepdims=True)
    big = m[...]
    w = w_ref[...].astype(F32)
    rec_ref[...] = big
    dg_ref[...] = rel[BINS:BINS + 1]
    db_ref[...] = jnp.sum(jnp.transpose(w * total), axis=0, keepdims=True)
    dsr_ref[...] = split_dot(rows[...], wr_ref[...], ((1,), (1,)), True)
    dsc_ref[...] = split_dot(cols_ref[...], wc_ref[...], ((1,), (1,)), True)


def finish(core, own, other, cols, wr, wc, w, nrows):
    f = lambda *s: jax.ShapeDtypeStruct(s, F32)
    vmem = pl.BlockSpec(memory_space=pltpu.VMEM)
    return pl.pallas_call(
        final_kernel,
        in_specs=[pl.BlockSpec(memory_space=pltpu.SMEM)] + [vmem] * 6,
        out_specs=[vmem] * 8,
        out_shape=[f(nrows, S), f(cols.shape[0], S), f(S, C), f(S, C), f(C, C), f(BINS, C), f(1, C), f(1, C)],
        scratch_shapes=[
            pltpu.VMEM((2, 16, CHUNK, C), F32),
            pltpu.VMEM((C, C), F32),
            pltpu.VMEM((nrows, C), F32),
            pltpu.VMEM((144, C), F32),
        ],
        compiler_params=pltpu.CompilerParams(vmem_limit_bytes=16 * 1024 * 1024),
        name="finish",
    )(core, own, other, cols, wr, wc, w)


def swap(a, axis, size, bit):
    return lax.ppermute(a, axis, [(i, i ^ bit) for i in range(size)])


def shards(cot, prev, single_rows, single_cols, w_row, w_col, w_rec, gain, bias, ids_rows, ids_cols):
    core = lax.axis_index("c").astype(jnp.int32).reshape(1)
    gain2, bias2 = gain.reshape(1, C), bias.reshape(1, C)
    send, keep, col_part, d_prev = local_reductions(
        core, cot, prev, w_rec, gain2, bias2, ids_rows, ids_cols, single_rows, single_cols
    )
    half = keep + swap(send, "c", 2, 1)
    chunks = lax.all_to_all(half, COLG, 0, 0)
    mine = jnp.sum(chunks, axis=0)
    z = jnp.concatenate([mine, col_part], axis=0)
    for axis, size, bit in (("x", 4, 1), ("x", 4, 3), ("zh", 2, 1)):
        z = z + swap(z, axis, size, bit)
    kept = lax.broadcasted_iota(jnp.int32, (CHUNK, 1), 0) // 4 == 1
    full = jnp.where(kept, mine, z[:CHUNK])
    col_sum = z[CHUNK:]
    own = lax.all_to_all(jnp.broadcast_to(full[None], (16, CHUNK, C)), COLG, 0, 0)
    other = swap(own, "c", 2, 1)
    dsr, dsc, dwr, dwc, rec, rel, dg, db = finish(core, own, other, col_sum, w_row, w_col, w_rec, cot.shape[0])
    return d_prev, dsr, dsc, dwr, dwc, rec, rel, dg.reshape(C), db.reshape(C)


def solution(mesh):
    fine = Mesh(mesh.devices.reshape(2, 4, 4, 4, 2), ("zh", "x", "y", "zl", "c"))
    row, col = ROW, COLG + ("c",)
    return jax.shard_map(
        shards,
        mesh=fine,
        in_specs=(
            P(row, col, None), P(row, col, None), P(row, None), P(col, None),
            P(), P(), P(), P(), P(), P(None, row), P(None, col),
        ),
        out_specs=(P(row, col, None), P(row, None), P(col, None), P(), P(), P(), P(), P(), P()),
        check_vma=False,
    )
```

```python
import functools

import jax
import jax.numpy as jnp
from jax import lax
from jax.experimental import pallas as pl
from jax.experimental.pallas import tpu as pltpu
from jax.sharding import Mesh, PartitionSpec as P

F32, BF16 = jnp.float32, jnp.bfloat16
C = 128
S = 384
BINS = 139
SUB = 16
CHUNK = 40
PARTS = 32
VMEM = 40 * 1024 * 1024
ROW = ("zh", "x")
COLG = ("y", "zl")


def dot(a, b, dims):
    return lax.dot_general(a, b, (dims, ((), ())), preferred_element_type=F32)


def split_dot(a, b, dims, split_left):
    x = a if split_left else b
    hi = x.astype(BF16)
    low = (x - hi.astype(F32)).astype(BF16)
    if split_left:
        return dot(hi, b, dims) + dot(low, b, dims)
    return dot(a, hi, dims) + dot(a, low, dims)


def reduce_kernel(cols, steps, rows, core_ref, cot_ref, prev_ref, w_ref, gain_ref, bias_ref, idr_ref, idc_ref, sr_hbm, sc_hbm,
                  send_ref, keep_ref, colp_ref, dprev_ref, acc, gains, gcol, bcol, rowp, colp, buf, sr_ref, sc_ref, sems):
    step = pl.program_id(0)
    fetch = [pltpu.make_async_copy(sr_hbm, sr_ref, sems.at[0]), pltpu.make_async_copy(sc_hbm, sc_ref, sems.at[1])]

    @pl.when(step == 0)
    def _():
        acc[...] = jnp.zeros_like(acc)
        gains[...] = jnp.zeros_like(gains)
        gcol[...] = jnp.transpose(jnp.broadcast_to(gain_ref[...], (C, C)))
        bcol[...] = jnp.transpose(jnp.broadcast_to(bias_ref[...], (C, C)))
        colp[...] = jnp.zeros_like(colp)
        for f in fetch:
            f.start()

    n = SUB * cols
    idr = idr_ref[...].astype(F32)
    idc = idc_ref[...].astype(F32)
    gain, bias = gcol[:, 0:1], bcol[:, 0:1]
    lane = lax.broadcasted_iota(jnp.int32, (SUB, idr.shape[1]), 1)
    sub = lax.broadcasted_iota(jnp.int32, (SUB, idr.shape[1]), 0)
    flat_lane = lax.broadcasted_iota(jnp.int32, (16, n), 1)
    flat_sub = lax.broadcasted_iota(jnp.int32, (16, n), 0)
    rowind = jnp.where((flat_lane >= flat_sub * cols) & (flat_lane < (flat_sub + 1) * cols), 1.0, 0.0).astype(BF16)

    eye = lax.broadcasted_iota(jnp.int32, (C, C), 0) == lax.broadcasted_iota(jnp.int32, (C, C), 1)
    centering = (jnp.where(eye, 1.0, 0.0) - 1.0 / C).astype(BF16)

    w = w_ref[...]
    lead = jnp.sum(w.astype(F32) * gcol[...], axis=0, keepdims=True) * (1.0 / C)
    lead_hi = lead.astype(BF16).astype(F32)
    sub16 = lax.broadcasted_iota(jnp.int32, (16, C), 0)
    extra = jnp.where(sub16 == 0, lead_hi, jnp.where(sub16 == 1, lead - lead_hi, 0.0))
    wide_w = jnp.concatenate([w, extra.astype(BF16)], axis=0)

    def mean(a):
        return jnp.sum(a, axis=0, keepdims=True) * (1.0 / C)

    for b in range(0, rows, SUB):
        first = step * rows + b
        cot = cot_ref[b:b + SUB].reshape(n, C)
        centered = dot(centering, prev_ref[b:b + SUB].reshape(n, C), ((1,), (1,)))
        rstd = lax.rsqrt(mean(centered * centered) + 1e-05)
        xhat = centered * rstd
        normed = (xhat * gain + bias).astype(BF16)
        y = dot(wide_w, cot, ((1,), (1,)))
        g = y[:C] * gain
        g_mean = y[C:C + 1] + y[C + 1:C + 2]
        gx = g * xhat
        share = gx[:, 0:C]
        for lo in range(C, n, C):
            share += gx[:, lo:lo + C]
        gains[...] += share
        res = (rstd * (g - g_mean - xhat * mean(gx))).astype(BF16)
        dprev_ref[b:b + SUB] = jnp.transpose(res).reshape(SUB, cols, C)
        mask = lane == sub + first
        di = [jnp.sum(jnp.where(mask, idr[k:k + 1], 0.0), axis=1, keepdims=True) for k in range(5)]
        dj = [idc[k:k + 1] for k in range(5)]
        same_chain = di[2] == dj[2]
        same_res = same_chain & (di[0] == dj[0])
        same_entity = di[3] == dj[3]
        r = jnp.where(same_chain, jnp.clip(di[0] - dj[0] + 32.0, 0.0, 64.0), 65.0)
        t = jnp.where(same_res, jnp.clip(di[1] - dj[1] + 32.0, 0.0, 64.0), 65.0)
        c = jnp.where(same_entity & jnp.logical_not(same_chain), jnp.clip(di[4] - dj[4] + 2.0, 0.0, 4.0), 5.0)
        packed = (r + 128.0 * t + 16384.0 * c).astype(jnp.int32) + jnp.where(same_entity, 1 << 18, 0)
        packed = jnp.concatenate([packed[s:s + 1] for s in range(SUB)], axis=1)
        r, t, c = packed & 127, ((packed >> 7) & 127) + 66, ((packed >> 14) & 15) + 133
        e = jnp.where(packed >= 1 << 18, 132, -1)

        def hot(lo, hi, *codes):
            q = lax.broadcasted_iota(jnp.int32, (hi - lo, n), 0) + lo
            hit = q == codes[0]
            for code in codes[1:]:
                hit = hit | (q == code)
            return jnp.where(hit, 1.0, 0.0).astype(BF16)

        left = jnp.concatenate(
            [normed, hot(0, 64, r), hot(64, 80, r, t), hot(80, 128, t), hot(128, 144, t, e, c), rowind], axis=0
        )
        out = dot(left, cot, ((1,), (0,)))
        acc[...] += out[:272]
        rowp[pl.ds(pl.multiple_of(first, SUB), SUB), :] = out[272:288]
        wide = cot_ref[b].astype(F32)
        for s in range(1, SUB):
            wide += cot_ref[b + s].astype(F32)
        colp[...] += wide

    @pl.when(step == steps - 1)
    def _():
        for f in fetch:
            f.wait()
        dwr = split_dot(sr_ref[...], rowp[...], ((0,), (0,)), False)
        dwc = split_dot(sc_ref[...], colp[...], ((0,), (0,)), False)
        acc[267:268] = jnp.sum(jnp.transpose(gains[...]), axis=0, keepdims=True) / gain_ref[...]
        total = acc[...]
        colp_ref[...] = colp[...]
        for k in range(PARTS):
            half, place = k // 16, k % 16
            buf[half, place, 0:4] = total[4 * k:4 * k + 4]
            buf[half, place, 4:8] = rowp[4 * k:4 * k + 4]
            lo, hi = 128 + 5 * k, min(128 + 5 * k + 5, 272)
            if lo < hi:
                buf[half, place, 8:8 + hi - lo] = total[lo:hi]
            pad = 8 + max(hi - lo, 0)
            buf[half, place, pad:16] = jnp.zeros((16 - pad, C), F32)
            buf[half, place, 16:28] = dwr[12 * k:12 * k + 12]
            buf[half, place, 28:40] = dwc[12 * k:12 * k + 12]
        core = core_ref[0]
        keep_ref[...] = buf[core]
        send_ref[...] = buf[1 - core]


def local_reductions(core, cot, prev, w, gain, bias, idr, idc, sr, sc, per=32):
    rows, cols = cot.shape[:2]
    steps = rows // per
    whole = lambda a: pl.BlockSpec(a.shape, lambda i: (0,) * a.ndim)
    block = pl.BlockSpec((per, cols, C), lambda i: (i, 0, 0))
    part = jax.ShapeDtypeStruct((16, CHUNK, C), F32)
    colo = jax.ShapeDtypeStruct((cols, C), F32)
    return pl.pallas_call(
        functools.partial(reduce_kernel, cols, steps, per),
        grid=(steps,),
        in_specs=[
            pl.BlockSpec(memory_space=pltpu.SMEM),
            block, block,
            whole(w), whole(gain), whole(bias), whole(idr), whole(idc),
            pl.BlockSpec(memory_space=pltpu.HBM), pl.BlockSpec(memory_space=pltpu.HBM),
        ],
        out_specs=[pl.BlockSpec(memory_space=pltpu.VMEM)] * 3 + [block],
        out_shape=[part, part, colo] + [jax.ShapeDtypeStruct(cot.shape, BF16)],
        scratch_shapes=[
            pltpu.VMEM((272, C), F32),
            pltpu.VMEM((C, C), F32),
            pltpu.VMEM((C, C), F32),
            pltpu.VMEM((C, C), F32),
            pltpu.VMEM((rows, C), F32),
            pltpu.VMEM((cols, C), F32),
            pltpu.VMEM((2, 16, CHUNK, C), F32),
            pltpu.VMEM(sr.shape, BF16),
            pltpu.VMEM(sc.shape, BF16),
            pltpu.SemaphoreType.DMA((2,)),
        ],
        compiler_params=pltpu.CompilerParams(vmem_limit_bytes=VMEM),
        name="local_reductions",
    )(core, *[pltpu.with_memory_space_constraint(a, pltpu.HBM) for a in (cot, prev, w, gain, bias, idr, idc, sr, sc)])


def final_kernel(core_ref, own_ref, other_ref, cols_ref, wr_ref, wc_ref, w_ref,
                 dsr_ref, dsc_ref, dwr_ref, dwc_ref, rec_ref, rel_ref, dg_ref, db_ref, buf, m, rows, rel):
    core = core_ref[0]
    buf[core] = own_ref[...]
    buf[1 - core] = other_ref[...]
    for k in range(PARTS):
        half, place = k // 16, k % 16
        m[4 * k:4 * k + 4] = buf[half, place, 0:4]
        rows[4 * k:4 * k + 4] = buf[half, place, 4:8]
        lo, hi = 5 * k, min(5 * k + 5, 144)
        if lo < hi:
            rel[lo:hi] = buf[half, place, 8:8 + hi - lo]
        dwr_ref[12 * k:12 * k + 12] = buf[half, place, 16:28]
        dwc_ref[12 * k:12 * k + 12] = buf[half, place, 28:40]
    rel_ref[...] = rel[0:BINS]
    total = jnp.sum(rel[133:139], axis=0, keepdims=True)
    big = m[...]
    w = w_ref[...].astype(F32)
    rec_ref[...] = big
    dg_ref[...] = rel[BINS:BINS + 1]
    db_ref[...] = jnp.sum(jnp.transpose(w * total), axis=0, keepdims=True)
    dsr_ref[...] = split_dot(rows[...], wr_ref[...], ((1,), (1,)), True)
    dsc_ref[...] = split_dot(cols_ref[...], wc_ref[...], ((1,), (1,)), True)


def finish(core, own, other, cols, wr, wc, w, nrows):
    f = lambda *s: jax.ShapeDtypeStruct(s, F32)
    vmem = pl.BlockSpec(memory_space=pltpu.VMEM)
    return pl.pallas_call(
        final_kernel,
        in_specs=[pl.BlockSpec(memory_space=pltpu.SMEM)] + [vmem] * 6,
        out_specs=[vmem] * 8,
        out_shape=[f(nrows, S), f(cols.shape[0], S), f(S, C), f(S, C), f(C, C), f(BINS, C), f(1, C), f(1, C)],
        scratch_shapes=[
            pltpu.VMEM((2, 16, CHUNK, C), F32),
            pltpu.VMEM((C, C), F32),
            pltpu.VMEM((nrows, C), F32),
            pltpu.VMEM((144, C), F32),
        ],
        compiler_params=pltpu.CompilerParams(vmem_limit_bytes=16 * 1024 * 1024),
        name="finish",
    )(core, own, other, cols, wr, wc, w)


def swap(a, axis, size, bit):
    return lax.ppermute(a, axis, [(i, i ^ bit) for i in range(size)])


def shards(cot, prev, single_rows, single_cols, w_row, w_col, w_rec, gain, bias, ids_rows, ids_cols):
    core = lax.axis_index("c").astype(jnp.int32).reshape(1)
    gain2, bias2 = gain.reshape(1, C), bias.reshape(1, C)
    send, keep, col_part, d_prev = local_reductions(
        core, cot, prev, w_rec, gain2, bias2, ids_rows, ids_cols, single_rows, single_cols
    )
    half = keep + swap(send, "c", 2, 1)
    chunks = lax.all_to_all(half, COLG, 0, 0)
    mine = jnp.sum(chunks, axis=0)
    z = jnp.concatenate([mine, col_part], axis=0)
    a, b, c = [swap(z, "x", 4, bit) for bit in (1, 3, 2)]
    z = (z + a) + (c + b)
    z = z + swap(z, "zh", 2, 1)
    kept = lax.broadcasted_iota(jnp.int32, (CHUNK, 1), 0) // 4 == 1
    full = jnp.where(kept, mine, z[:CHUNK])
    col_sum = z[CHUNK:]
    own = lax.all_to_all(jnp.broadcast_to(full[None], (16, CHUNK, C)), COLG, 0, 0)
    other = swap(own, "c", 2, 1)
    dsr, dsc, dwr, dwc, rec, rel, dg, db = finish(core, own, other, col_sum, w_row, w_col, w_rec, cot.shape[0])
    return d_prev, dsr, dsc, dwr, dwc, rec, rel, dg.reshape(C), db.reshape(C)


def solution(mesh):
    fine = Mesh(mesh.devices.reshape(2, 4, 4, 4, 2), ("zh", "x", "y", "zl", "c"))
    row, col = ROW, COLG + ("c",)
    return jax.shard_map(
        shards,
        mesh=fine,
        in_specs=(
            P(row, col, None), P(row, col, None), P(row, None), P(col, None),
            P(), P(), P(), P(), P(), P(None, row), P(None, col),
        ),
        out_specs=(P(row, col, None), P(row, None), P(col, None), P(), P(), P(), P(), P(), P()),
        check_vma=False,
    )
```

```python
import functools

import jax
import jax.numpy as jnp
from jax import lax
from jax.experimental import pallas as pl
from jax.experimental.pallas import tpu as pltpu
from jax.sharding import Mesh, PartitionSpec as P

F32, BF16 = jnp.float32, jnp.bfloat16
C = 128
S = 384
BINS = 139
SUB = 16
CHUNK = 36
ROWS_AT, COLS_AT = 16, 28
WIDE = CHUNK + COLS_AT
PARTS = 32
PLANE, LINE = 16, 8
VMEM = 40 * 1024 * 1024
XY, Z = ("x", "y"), ("zh", "zl")
ROW, COL = ("zh", "x"), ("y", "zl", "c")


def dot(a, b, dims):
    return lax.dot_general(a, b, (dims, ((), ())), preferred_element_type=F32)


def split_dot(a, b, dims, split_left):
    x = a if split_left else b
    hi = x.astype(BF16)
    low = (x - hi.astype(F32)).astype(BF16)
    if split_left:
        return dot(hi, b, dims) + dot(low, b, dims)
    return dot(a, hi, dims) + dot(a, low, dims)


def reduce_kernel(cols, rows, cot_hbm, prev_hbm, w_hbm, gain_hbm, bias_hbm, idr_hbm, idc_hbm, sr_hbm, sc_hbm,
                  send_ref, keep_ref, colp_ref, dprev_hbm,
                  cot_ref, prev_ref, dprev_ref, w_ref, gain_ref, bias_ref, idr_ref, idc_ref, sr_ref, sc_ref,
                  acc, gains, gcol, bcol, rowp, buf, small_sems, in_sems, out_sems):
    units = rows // SUB
    small = [
        pltpu.make_async_copy(src, dst, small_sems.at[k])
        for k, (src, dst) in enumerate((
            (gain_hbm, gain_ref), (bias_hbm, bias_ref), (w_hbm, w_ref), (idr_hbm, idr_ref), (idc_hbm, idc_ref),
            (sr_hbm, sr_ref), (sc_hbm, sc_ref),
        ))
    ]

    def part(u):
        return pl.ds(pl.multiple_of(u * SUB, SUB), SUB)

    def fetch(u):
        return [
            pltpu.make_async_copy(src.at[part(u)], dst.at[part(u)], in_sems.at[k, u])
            for k, (src, dst) in enumerate(((prev_hbm, prev_ref), (cot_hbm, cot_ref)))
        ]

    def put(u):
        return pltpu.make_async_copy(dprev_ref.at[part(u)], dprev_hbm.at[part(u)], out_sems.at[u])

    for copy in small[:5] + fetch(0) + fetch(1) + small[5:]:
        copy.start()
    acc[...] = jnp.zeros_like(acc)
    gains[...] = jnp.zeros_like(gains)
    colp_ref[...] = jnp.zeros_like(colp_ref)
    for copy in small[:5]:
        copy.wait()
    gcol[...] = jnp.transpose(jnp.broadcast_to(gain_ref[...], (C, C)))
    bcol[...] = jnp.transpose(jnp.broadcast_to(bias_ref[...], (C, C)))

    n = SUB * cols
    idr = idr_ref[...].astype(F32)
    idc = idc_ref[...].astype(F32)
    gain, bias = gcol[:, 0:1], bcol[:, 0:1]
    lane = lax.broadcasted_iota(jnp.int32, (SUB, idr.shape[1]), 1)
    sub = lax.broadcasted_iota(jnp.int32, (SUB, idr.shape[1]), 0)
    flat_lane = lax.broadcasted_iota(jnp.int32, (16, n), 1)
    flat_sub = lax.broadcasted_iota(jnp.int32, (16, n), 0)
    rowind = jnp.where((flat_lane >= flat_sub * cols) & (flat_lane < (flat_sub + 1) * cols), 1.0, 0.0).astype(BF16)

    eye = lax.broadcasted_iota(jnp.int32, (C, C), 0) == lax.broadcasted_iota(jnp.int32, (C, C), 1)
    centering = (jnp.where(eye, 1.0, 0.0) - 1.0 / C).astype(BF16)

    w = w_ref[...]
    lead = jnp.sum(w.astype(F32) * gcol[...], axis=0, keepdims=True) * (1.0 / C)
    lead_hi = lead.astype(BF16).astype(F32)
    sub16 = lax.broadcasted_iota(jnp.int32, (16, C), 0)
    extra = jnp.where(sub16 == 0, lead_hi, jnp.where(sub16 == 1, lead - lead_hi, 0.0))
    wide_w = jnp.concatenate([w, extra.astype(BF16)], axis=0)

    def mean(a):
        return jnp.sum(a, axis=0, keepdims=True) * (1.0 / C)

    @pl.loop(0, units, unroll=8)
    def _(u):
        for copy in fetch(u):
            copy.wait()

        @pl.when(u + 2 < units)
        def _():
            for copy in fetch(u + 2):
                copy.start()

        first = u * SUB
        here = part(u)
        cot = cot_ref[here].reshape(n, C)
        centered = dot(centering, prev_ref[here].reshape(n, C), ((1,), (1,)))
        rstd = lax.rsqrt(mean(centered * centered) + 1e-05)
        xhat = centered * rstd
        normed = (xhat * gain + bias).astype(BF16)
        y = dot(wide_w, cot, ((1,), (1,)))
        g = y[:C] * gain
        g_mean = y[C:C + 1] + y[C + 1:C + 2]
        gx = g * xhat
        share = gx[:, 0:C]
        for lo in range(C, n, C):
            share += gx[:, lo:lo + C]
        gains[...] += share
        res = (rstd * (g - g_mean - xhat * mean(gx))).astype(BF16)
        dprev_ref[here] = jnp.transpose(res).reshape(SUB, cols, C)
        put(u).start()
        mask = lane == sub + first
        di = [jnp.sum(jnp.where(mask, idr[k:k + 1], 0.0), axis=1, keepdims=True) for k in range(5)]
        dj = [idc[k:k + 1] for k in range(5)]
        same_chain = di[2] == dj[2]
        same_res = same_chain & (di[0] == dj[0])
        same_entity = di[3] == dj[3]
        r = jnp.where(same_chain, jnp.clip(di[0] - dj[0] + 32.0, 0.0, 64.0), 65.0)
        t = jnp.where(same_res, jnp.clip(di[1] - dj[1] + 32.0, 0.0, 64.0), 65.0)
        c = jnp.where(same_entity & jnp.logical_not(same_chain), jnp.clip(di[4] - dj[4] + 2.0, 0.0, 4.0), 5.0)
        packed = (r + 128.0 * t + 16384.0 * c).astype(jnp.int32) + jnp.where(same_entity, 1 << 18, 0)
        packed = jnp.concatenate([packed[s:s + 1] for s in range(SUB)], axis=1)
        r, t, c = packed & 127, ((packed >> 7) & 127) + 66, ((packed >> 14) & 15) + 133
        e = jnp.where(packed >= 1 << 18, 132, -1)

        def hot(lo, hi, *codes):
            q = lax.broadcasted_iota(jnp.int32, (hi - lo, n), 0) + lo
            hit = q == codes[0]
            for code in codes[1:]:
                hit = hit | (q == code)
            return jnp.where(hit, 1.0, 0.0).astype(BF16)

        left = jnp.concatenate(
            [normed, hot(0, 64, r), hot(64, 80, r, t), hot(80, 128, t), hot(128, 144, t, e, c), rowind], axis=0
        )
        out = dot(left, cot, ((1,), (0,)))
        acc[...] += out[:272]
        rowp[here, :] = out[272:288]
        wide = cot[:cols].astype(F32)
        for s in range(1, SUB):
            wide += cot[s * cols:(s + 1) * cols].astype(F32)
        colp_ref[...] += wide

    for copy in small[5:]:
        copy.wait()
    dwr = split_dot(sr_ref[...], rowp[...], ((0,), (0,)), False)
    dwc = split_dot(sc_ref[...], colp_ref[...], ((0,), (0,)), False)
    acc[267:268] = jnp.sum(jnp.transpose(gains[...]), axis=0, keepdims=True) / gain_ref[...]
    total = acc[...]
    for k in range(PARTS):
        half, at = k // PLANE, k % PLANE * CHUNK
        buf[half, at:at + 12] = dwr[12 * k:12 * k + 12]
        buf[half, at + 12:at + 24] = dwc[12 * k:12 * k + 12]
        buf[half, at + 24:at + 28] = total[4 * k:4 * k + 4]
        lo, hi = 128 + 5 * k, min(128 + 5 * k + 5, 272)
        if lo < hi:
            buf[half, at + 28:at + 28 + hi - lo] = total[lo:hi]
        pad = 28 + max(hi - lo, 0)
        buf[half, at + pad:at + CHUNK] = jnp.zeros((CHUNK - pad, C), F32)
    for half in range(2):
        buf[half, PLANE * CHUNK:] = rowp[half * rows // 2:(half + 1) * rows // 2]
    core = lax.axis_index("c")
    keep_ref[...] = buf[core]
    send_ref[...] = buf[1 - core]

    @pl.loop(0, units)
    def _(u):
        put(u).wait()


def local_reductions(cot, prev, w, gain, bias, idr, idc, sr, sc):
    rows, cols = cot.shape[:2]
    units = rows // SUB
    part = jax.ShapeDtypeStruct((PLANE * CHUNK + rows // 2, C), F32)
    hbm, vmem = pl.BlockSpec(memory_space=pltpu.HBM), pl.BlockSpec(memory_space=pltpu.VMEM)
    same = lambda a: pltpu.VMEM(a.shape, a.dtype)
    arrays = (cot, prev, w, gain, bias, idr, idc, sr, sc)
    return pl.pallas_call(
        functools.partial(reduce_kernel, cols, rows),
        in_specs=[hbm] * 9,
        out_specs=[vmem, vmem, vmem, hbm],
        out_shape=[part, part, jax.ShapeDtypeStruct((cols, C), F32), jax.ShapeDtypeStruct(cot.shape, BF16)],
        scratch_shapes=[same(cot), same(prev), same(cot)] + [same(a) for a in arrays[2:]] + [
            pltpu.VMEM((272, C), F32),
            pltpu.VMEM((C, C), F32),
            pltpu.VMEM((C, C), F32),
            pltpu.VMEM((C, C), F32),
            pltpu.VMEM((rows, C), F32),
            pltpu.VMEM((2,) + part.shape, F32),
            pltpu.SemaphoreType.DMA((7,)),
            pltpu.SemaphoreType.DMA((2, units)),
            pltpu.SemaphoreType.DMA((units,)),
        ],
        compiler_params=pltpu.CompilerParams(vmem_limit_bytes=VMEM),
        name="local_reductions",
    )(*[pltpu.with_memory_space_constraint(a, pltpu.HBM) for a in arrays])


def plane_kernel(keep_ref, got_ref, colp_ref, out_ref, mine_ref):
    x, y = lax.axis_index("x"), lax.axis_index("y")
    for k in range(PLANE):
        out_ref[k, 0:CHUNK] = keep_ref[CHUNK * k:CHUNK * (k + 1)] + got_ref[CHUNK * k:CHUNK * (k + 1)]
        out_ref[k, CHUNK:] = jnp.zeros((COLS_AT, C), F32)
    for j in range(4):
        at = PLANE * CHUNK + ROWS_AT * j
        part = keep_ref[at:at + ROWS_AT] + got_ref[at:at + ROWS_AT]
        out_ref[4 * x + j, CHUNK:CHUNK + ROWS_AT] = part

        @pl.when(y == j)
        def _():
            mine_ref[...] = part

    for j in range(4):
        out_ref[4 * j + y, CHUNK:] = colp_ref[COLS_AT * j:COLS_AT * (j + 1)]


def line_kernel(r_ref, row_ref, out_ref, mine_ref):
    x, y, zh, zl = [lax.axis_index(a) for a in ("x", "y", "zh", "zl")]
    total = r_ref[0, 0:CHUNK]
    for k in range(1, PLANE):
        total += r_ref[k, 0:CHUNK]
    rows = jnp.zeros((ROWS_AT, C), F32)
    cols = jnp.zeros((COLS_AT, C), F32)
    for j in range(4):
        rows += jnp.where(j == y, row_ref[...], r_ref[4 * x + j, CHUNK:CHUNK + ROWS_AT])
        cols += r_ref[4 * j + y, CHUNK:]
    for k in range(LINE):
        out_ref[k, 0:CHUNK] = total
        out_ref[k, CHUNK:] = jnp.zeros((COLS_AT, C), F32)
    out_ref[4 * (1 - zh) + zl, CHUNK:] = cols
    for j in range(4):
        out_ref[4 * zh + j, CHUNK:CHUNK + ROWS_AT] = rows
    mine_ref[...] = cols


def spread_kernel(r_ref, col_ref, out_ref, mine_ref):
    x, y, zh, zl = [lax.axis_index(a) for a in ("x", "y", "zh", "zl")]
    total = r_ref[0, 0:CHUNK]
    for k in range(1, LINE):
        total += r_ref[k, 0:CHUNK]
    rows = r_ref[4 * zh, CHUNK:CHUNK + ROWS_AT]
    for j in range(1, 4):
        rows += r_ref[4 * zh + j, CHUNK:CHUNK + ROWS_AT]
    cols = col_ref[...] + r_ref[4 * (1 - zh) + zl, CHUNK:]
    for k in range(PLANE):
        out_ref[k, 0:CHUNK] = total
        out_ref[k, CHUNK:] = jnp.zeros((COLS_AT, C), F32)
    for j in range(4):
        out_ref[4 * j + y, CHUNK:] = cols
    for j in range(4):
        out_ref[4 * x + j, CHUNK:CHUNK + ROWS_AT] = rows
    mine_ref[...] = cols


def glue(kernel, name, parts, mine, *args):
    vmem = pl.BlockSpec(memory_space=pltpu.VMEM)
    return pl.pallas_call(
        kernel,
        in_specs=[vmem] * len(args),
        out_specs=[vmem] * 2,
        out_shape=[jax.ShapeDtypeStruct((parts, WIDE, C), F32), jax.ShapeDtypeStruct((mine, C), F32)],
        compiler_params=pltpu.CompilerParams(vmem_limit_bytes=16 * 1024 * 1024),
        name=name,
    )(*args)


def final_kernel(own_ref, other_ref, col_ref, wr_ref, wc_ref, w_ref,
                 dsr_ref, dsc_ref, dwr_ref, dwc_ref, rec_ref, rel_ref, dg_ref, db_ref, buf, m, rows, cols, rel):
    core, x, y = [lax.axis_index(a) for a in ("c", "x", "y")]
    buf[core] = own_ref[...]
    buf[1 - core] = other_ref[...]
    for k in range(PARTS):
        half, place = k // PLANE, k % PLANE
        dwr_ref[12 * k:12 * k + 12] = buf[half, place, 0:12]
        dwc_ref[12 * k:12 * k + 12] = buf[half, place, 12:24]
        m[4 * k:4 * k + 4] = buf[half, place, 24:28]
        lo, hi = 5 * k, min(5 * k + 5, 144)
        if lo < hi:
            rel[lo:hi] = buf[half, place, 28:28 + hi - lo]
    for half in range(2):
        for j in range(4):
            at = ROWS_AT * (4 * half + j)
            rows[at:at + ROWS_AT] = buf[half, 4 * x + j, CHUNK:CHUNK + ROWS_AT]
    for j in range(4):
        cols[COLS_AT * j:COLS_AT * (j + 1)] = jnp.where(j == x, col_ref[...], own_ref[4 * j + y, CHUNK:])
    rel_ref[...] = rel[0:BINS]
    total = jnp.sum(rel[133:139], axis=0, keepdims=True)
    w = w_ref[...].astype(F32)
    rec_ref[...] = m[...]
    dg_ref[...] = rel[BINS:BINS + 1]
    db_ref[...] = jnp.sum(jnp.transpose(w * total), axis=0, keepdims=True)
    dsr_ref[...] = split_dot(rows[...], wr_ref[...], ((1,), (1,)), True)
    dsc_ref[...] = split_dot(cols[...], wc_ref[...], ((1,), (1,)), True)


def finish(own, other, col, wr, wc, w, nrows, ncols):
    f = lambda *s: jax.ShapeDtypeStruct(s, F32)
    vmem = pl.BlockSpec(memory_space=pltpu.VMEM)
    return pl.pallas_call(
        final_kernel,
        in_specs=[vmem] * 6,
        out_specs=[vmem] * 8,
        out_shape=[f(nrows, S), f(ncols, S), f(S, C), f(S, C), f(C, C), f(BINS, C), f(1, C), f(1, C)],
        scratch_shapes=[
            pltpu.VMEM((2, PLANE, WIDE, C), F32),
            pltpu.VMEM((C, C), F32),
            pltpu.VMEM((nrows, C), F32),
            pltpu.VMEM((ncols, C), F32),
            pltpu.VMEM((144, C), F32),
        ],
        compiler_params=pltpu.CompilerParams(vmem_limit_bytes=16 * 1024 * 1024),
        name="finish",
    )(own, other, col, wr, wc, w)


def swap(a):
    return lax.ppermute(a, "c", [(0, 1), (1, 0)])


def shards(cot, prev, single_rows, single_cols, w_row, w_col, w_rec, gain, bias, ids_rows, ids_cols):
    nrows, ncols = cot.shape[:2]
    gain2, bias2 = gain.reshape(1, C), bias.reshape(1, C)
    send, keep, col_part, d_prev = local_reductions(
        cot, prev, w_rec, gain2, bias2, ids_rows, ids_cols, single_rows, single_cols
    )
    shares, row_mine = glue(plane_kernel, "plane", PLANE, ROWS_AT, keep, swap(send), col_part)
    shares, col_mine = glue(line_kernel, "line", LINE, COLS_AT, lax.all_to_all(shares, XY, 0, 0), row_mine)
    shares, col_mine = glue(spread_kernel, "spread", PLANE, COLS_AT, lax.all_to_all(shares, Z, 0, 0), col_mine)
    own = lax.all_to_all(shares, XY, 0, 0)
    dsr, dsc, dwr, dwc, rec, rel, dg, db = finish(own, swap(own), col_mine, w_row, w_col, w_rec, nrows, ncols)
    return d_prev, dsr, dsc, dwr, dwc, rec, rel, dg.reshape(C), db.reshape(C)


def solution(mesh):
    fine = Mesh(mesh.devices.reshape(2, 4, 4, 4, 2), ("zh", "x", "y", "zl", "c"))
    return jax.shard_map(
        shards,
        mesh=fine,
        in_specs=(
            P(ROW, COL, None), P(ROW, COL, None), P(ROW, None), P(COL, None),
            P(), P(), P(), P(), P(), P(None, ROW), P(None, COL),
        ),
        out_specs=(P(ROW, COL, None), P(ROW, None), P(COL, None), P(), P(), P(), P(), P(), P()),
        check_vma=False,
    )
```

```python
import functools

import jax
import jax.numpy as jnp
from jax import lax
from jax.experimental import pallas as pl
from jax.experimental.pallas import tpu as pltpu
from jax.sharding import Mesh, PartitionSpec as P

F32, BF16 = jnp.float32, jnp.bfloat16
C = 128
S = 384
BINS = 139
SUB = 16
SHARED = 33
ROWS_AT, COLS_AT = 4, 7
CHUNK = SHARED + ROWS_AT
WIDE = CHUNK + COLS_AT
PARTS = 32
PLANE, LINE = 16, 8
VMEM = 40 * 1024 * 1024
XY, Z = ("x", "y"), ("zh", "zl")
ROW, COL = ("zh", "x"), ("y", "zl", "c")


def dot(a, b, dims):
    return lax.dot_general(a, b, (dims, ((), ())), preferred_element_type=F32)


def split_dot(a, b, dims, split_left):
    x = a if split_left else b
    hi = x.astype(BF16)
    low = (x - hi.astype(F32)).astype(BF16)
    if split_left:
        return dot(hi, b, dims) + dot(low, b, dims)
    return dot(a, hi, dims) + dot(a, low, dims)


def reduce_kernel(cols, rows, cot_hbm, prev_hbm, w_hbm, gain_hbm, bias_hbm, idr_hbm, idc_hbm, sr_hbm, sc_hbm,
                  send_ref, keep_ref, colp_ref, dprev_hbm,
                  cot_ref, prev_ref, dprev_ref, w_ref, gain_ref, bias_ref, idr_ref, idc_ref, sr_ref, sc_ref,
                  acc, gains, gcol, bcol, rowp, buf, small_sems, in_sems, out_sems):
    units = rows // SUB
    small = [
        pltpu.make_async_copy(src, dst, small_sems.at[k])
        for k, (src, dst) in enumerate((
            (gain_hbm, gain_ref), (bias_hbm, bias_ref), (w_hbm, w_ref), (idr_hbm, idr_ref), (idc_hbm, idc_ref),
            (sr_hbm, sr_ref), (sc_hbm, sc_ref),
        ))
    ]

    def part(u):
        return pl.ds(pl.multiple_of(u * SUB, SUB), SUB)

    def fetch(u):
        return [
            pltpu.make_async_copy(src.at[part(u)], dst.at[part(u)], in_sems.at[k, u])
            for k, (src, dst) in enumerate(((prev_hbm, prev_ref), (cot_hbm, cot_ref)))
        ]

    def put(u):
        return pltpu.make_async_copy(dprev_ref.at[part(u)], dprev_hbm.at[part(u)], out_sems.at[u])

    for copy in small[:5] + fetch(0) + fetch(1) + small[5:]:
        copy.start()
    acc[...] = jnp.zeros_like(acc)
    gains[...] = jnp.zeros_like(gains)
    colp_ref[...] = jnp.zeros_like(colp_ref)
    for copy in small[:5]:
        copy.wait()
    gcol[...] = jnp.transpose(jnp.broadcast_to(gain_ref[...], (C, C)))
    bcol[...] = jnp.transpose(jnp.broadcast_to(bias_ref[...], (C, C)))

    n = SUB * cols
    idr = idr_ref[...].astype(F32)
    idc = idc_ref[...].astype(F32)
    gain, bias = gcol[:, 0:1], bcol[:, 0:1]
    lane = lax.broadcasted_iota(jnp.int32, (SUB, idr.shape[1]), 1)
    sub = lax.broadcasted_iota(jnp.int32, (SUB, idr.shape[1]), 0)
    flat_lane = lax.broadcasted_iota(jnp.int32, (16, n), 1)
    flat_sub = lax.broadcasted_iota(jnp.int32, (16, n), 0)
    rowind = jnp.where((flat_lane >= flat_sub * cols) & (flat_lane < (flat_sub + 1) * cols), 1.0, 0.0).astype(BF16)

    eye = lax.broadcasted_iota(jnp.int32, (C, C), 0) == lax.broadcasted_iota(jnp.int32, (C, C), 1)
    centering = (jnp.where(eye, 1.0, 0.0) - 1.0 / C).astype(BF16)

    w = w_ref[...]
    lead = jnp.sum(w.astype(F32) * gcol[...], axis=0, keepdims=True) * (1.0 / C)
    lead_hi = lead.astype(BF16).astype(F32)
    sub16 = lax.broadcasted_iota(jnp.int32, (16, C), 0)
    extra = jnp.where(sub16 == 0, lead_hi, jnp.where(sub16 == 1, lead - lead_hi, 0.0))
    wide_w = jnp.concatenate([w, extra.astype(BF16)], axis=0)

    def mean(a):
        return jnp.sum(a, axis=0, keepdims=True) * (1.0 / C)

    @pl.loop(0, units, unroll=8)
    def _(u):
        for copy in fetch(u):
            copy.wait()

        @pl.when(u + 2 < units)
        def _():
            for copy in fetch(u + 2):
                copy.start()

        first = u * SUB
        here = part(u)
        cot = cot_ref[here].reshape(n, C)
        centered = dot(centering, prev_ref[here].reshape(n, C), ((1,), (1,)))
        rstd = lax.rsqrt(mean(centered * centered) + 1e-05)
        xhat = centered * rstd
        normed = (xhat * gain + bias).astype(BF16)
        y = dot(wide_w, cot, ((1,), (1,)))
        g = y[:C] * gain
        g_mean = y[C:C + 1] + y[C + 1:C + 2]
        gx = g * xhat
        share = gx[:, 0:C]
        for lo in range(C, n, C):
            share += gx[:, lo:lo + C]
        gains[...] += share
        res = (rstd * (g - g_mean - xhat * mean(gx))).astype(BF16)
        dprev_ref[here] = jnp.transpose(res).reshape(SUB, cols, C)
        put(u).start()
        mask = lane == sub + first
        di = [jnp.sum(jnp.where(mask, idr[k:k + 1], 0.0), axis=1, keepdims=True) for k in range(5)]
        dj = [idc[k:k + 1] for k in range(5)]
        same_chain = di[2] == dj[2]
        same_res = same_chain & (di[0] == dj[0])
        same_entity = di[3] == dj[3]
        r = jnp.where(same_chain, jnp.clip(di[0] - dj[0] + 32.0, 0.0, 64.0), 65.0)
        t = jnp.where(same_res, jnp.clip(di[1] - dj[1] + 32.0, 0.0, 64.0), 65.0)
        c = jnp.where(same_entity & jnp.logical_not(same_chain), jnp.clip(di[4] - dj[4] + 2.0, 0.0, 4.0), 5.0)
        packed = (r + 128.0 * t + 16384.0 * c).astype(jnp.int32) + jnp.where(same_entity, 1 << 18, 0)
        packed = jnp.concatenate([packed[s:s + 1] for s in range(SUB)], axis=1)
        r, t, c = packed & 127, ((packed >> 7) & 127) + 66, ((packed >> 14) & 15) + 133
        e = jnp.where(packed >= 1 << 18, 132, -1)

        def hot(lo, hi, *codes):
            q = lax.broadcasted_iota(jnp.int32, (hi - lo, n), 0) + lo
            hit = q == codes[0]
            for code in codes[1:]:
                hit = hit | (q == code)
            return jnp.where(hit, 1.0, 0.0).astype(BF16)

        left = jnp.concatenate(
            [normed, hot(0, 64, r), hot(64, 80, r, t), hot(80, 128, t), hot(128, 144, t, e, c), rowind], axis=0
        )
        out = dot(left, cot, ((1,), (0,)))
        acc[...] += out[:272]
        rowp[here, :] = out[272:288]
        wide = cot[:cols].astype(F32)
        for s in range(1, SUB):
            wide += cot[s * cols:(s + 1) * cols].astype(F32)
        colp_ref[...] += wide

    for copy in small[5:]:
        copy.wait()
    dwr = split_dot(sr_ref[...], rowp[...], ((0,), (0,)), False)
    dwc = split_dot(sc_ref[...], colp_ref[...], ((0,), (0,)), False)
    acc[267:268] = jnp.sum(jnp.transpose(gains[...]), axis=0, keepdims=True) / gain_ref[...]
    total = acc[...]
    for k in range(PARTS):
        half, at = k // PLANE, k % PLANE * CHUNK
        buf[half, at:at + 12] = dwr[12 * k:12 * k + 12]
        buf[half, at + 12:at + 24] = dwc[12 * k:12 * k + 12]
        buf[half, at + 24:at + 28] = total[4 * k:4 * k + 4]
        lo, hi = 128 + 5 * k, min(128 + 5 * k + 5, 272)
        if lo < hi:
            buf[half, at + 28:at + 28 + hi - lo] = total[lo:hi]
        if hi - lo < 5:
            buf[half, at + 28 + max(hi - lo, 0):at + SHARED] = jnp.zeros((5 - max(hi - lo, 0), C), F32)
        buf[half, at + SHARED:at + CHUNK] = rowp[ROWS_AT * k:ROWS_AT * (k + 1)]
    core = lax.axis_index("c")
    keep_ref[...] = buf[core]
    send_ref[...] = buf[1 - core]

    @pl.loop(0, units)
    def _(u):
        put(u).wait()


def local_reductions(cot, prev, w, gain, bias, idr, idc, sr, sc):
    rows, cols = cot.shape[:2]
    units = rows // SUB
    part = jax.ShapeDtypeStruct((PLANE * CHUNK, C), F32)
    hbm, vmem = pl.BlockSpec(memory_space=pltpu.HBM), pl.BlockSpec(memory_space=pltpu.VMEM)
    same = lambda a: pltpu.VMEM(a.shape, a.dtype)
    arrays = (cot, prev, w, gain, bias, idr, idc, sr, sc)
    return pl.pallas_call(
        functools.partial(reduce_kernel, cols, rows),
        in_specs=[hbm] * 9,
        out_specs=[vmem, vmem, vmem, hbm],
        out_shape=[part, part, jax.ShapeDtypeStruct((cols, C), F32), jax.ShapeDtypeStruct(cot.shape, BF16)],
        scratch_shapes=[same(cot), same(prev), same(cot)] + [same(a) for a in arrays[2:]] + [
            pltpu.VMEM((272, C), F32),
            pltpu.VMEM((C, C), F32),
            pltpu.VMEM((C, C), F32),
            pltpu.VMEM((C, C), F32),
            pltpu.VMEM((rows, C), F32),
            pltpu.VMEM((2,) + part.shape, F32),
            pltpu.SemaphoreType.DMA((7,)),
            pltpu.SemaphoreType.DMA((2, units)),
            pltpu.SemaphoreType.DMA((units,)),
        ],
        compiler_params=pltpu.CompilerParams(vmem_limit_bytes=VMEM),
        name="local_reductions",
    )(*[pltpu.with_memory_space_constraint(a, pltpu.HBM) for a in arrays])


def plane_kernel(keep_ref, got_ref, colp_ref, out_ref):
    for k in range(PLANE):
        at = slice(CHUNK * k, CHUNK * (k + 1))
        out_ref[k, 0:CHUNK] = keep_ref[at] + got_ref[at]
        out_ref[k, CHUNK:] = colp_ref[COLS_AT * k:COLS_AT * (k + 1)]


def line_kernel(r_ref, out_ref, mine_ref):
    zh, zl = lax.axis_index("zh"), lax.axis_index("zl")
    total = r_ref[0, 0:SHARED]
    for k in range(1, PLANE):
        total += r_ref[k, 0:SHARED]
    for i in range(4):
        part = r_ref[i, CHUNK:]
        for j in range(1, 4):
            part += r_ref[4 * j + i, CHUNK:]
        mine_ref[COLS_AT * i:COLS_AT * (i + 1)] = part
    for k in range(LINE):
        out_ref[k, 0:SHARED] = total
        out_ref[k, SHARED:] = jnp.zeros((4 * COLS_AT, C), F32)
    for i in range(4):
        part = r_ref[4 * i, SHARED:CHUNK]
        for j in range(1, 4):
            part += r_ref[4 * i + j, SHARED:CHUNK]
        at = SHARED + ROWS_AT * i
        for j in range(4):
            out_ref[4 * zh + j, at:at + ROWS_AT] = part
    out_ref[4 * (1 - zh) + zl, SHARED:] = mine_ref[...]


def spread_kernel(r_ref, mine_ref, out_ref):
    zh, zl = lax.axis_index("zh"), lax.axis_index("zl")
    total = r_ref[0, 0:SHARED]
    for k in range(1, LINE):
        total += r_ref[k, 0:SHARED]
    rows = r_ref[4 * zh, SHARED:SHARED + 4 * ROWS_AT]
    for j in range(1, 4):
        rows += r_ref[4 * zh + j, SHARED:SHARED + 4 * ROWS_AT]
    cols = mine_ref[...] + r_ref[4 * (1 - zh) + zl, SHARED:]
    for k in range(PLANE):
        i, j = k // 4, k % 4
        out_ref[k, 0:SHARED] = total
        out_ref[k, SHARED:CHUNK] = rows[ROWS_AT * i:ROWS_AT * (i + 1)]
        out_ref[k, CHUNK:] = cols[COLS_AT * j:COLS_AT * (j + 1)]


def glue(kernel, name, outs, *args):
    vmem = pl.BlockSpec(memory_space=pltpu.VMEM)
    return pl.pallas_call(
        kernel,
        in_specs=[vmem] * len(args),
        out_specs=[vmem] * len(outs),
        out_shape=[jax.ShapeDtypeStruct(shape + (C,), F32) for shape in outs],
        compiler_params=pltpu.CompilerParams(vmem_limit_bytes=16 * 1024 * 1024),
        name=name,
    )(*args)


def final_kernel(own_ref, other_ref, wr_ref, wc_ref, w_ref,
                 dsr_ref, dsc_ref, dwr_ref, dwc_ref, rec_ref, rel_ref, dg_ref, db_ref, buf, m, rows, cols, rel):
    core = lax.axis_index("c")
    buf[core] = own_ref[...]
    buf[1 - core] = other_ref[...]
    for k in range(PARTS):
        half, place = k // PLANE, k % PLANE
        dwr_ref[12 * k:12 * k + 12] = buf[half, place, 0:12]
        dwc_ref[12 * k:12 * k + 12] = buf[half, place, 12:24]
        m[4 * k:4 * k + 4] = buf[half, place, 24:28]
        lo, hi = 5 * k, min(5 * k + 5, 144)
        if lo < hi:
            rel[lo:hi] = buf[half, place, 28:28 + hi - lo]
        rows[ROWS_AT * k:ROWS_AT * (k + 1)] = buf[half, place, SHARED:CHUNK]
    for k in range(PLANE):
        cols[COLS_AT * k:COLS_AT * (k + 1)] = own_ref[k, CHUNK:]
    rel_ref[...] = rel[0:BINS]
    total = jnp.sum(rel[133:139], axis=0, keepdims=True)
    w = w_ref[...].astype(F32)
    rec_ref[...] = m[...]
    dg_ref[...] = rel[BINS:BINS + 1]
    db_ref[...] = jnp.sum(jnp.transpose(w * total), axis=0, keepdims=True)
    dsr_ref[...] = split_dot(rows[...], wr_ref[...], ((1,), (1,)), True)
    dsc_ref[...] = split_dot(cols[...], wc_ref[...], ((1,), (1,)), True)


def finish(own, other, wr, wc, w, nrows, ncols):
    f = lambda *s: jax.ShapeDtypeStruct(s, F32)
    vmem = pl.BlockSpec(memory_space=pltpu.VMEM)
    return pl.pallas_call(
        final_kernel,
        in_specs=[vmem] * 5,
        out_specs=[vmem] * 8,
        out_shape=[f(nrows, S), f(ncols, S), f(S, C), f(S, C), f(C, C), f(BINS, C), f(1, C), f(1, C)],
        scratch_shapes=[
            pltpu.VMEM((2, PLANE, WIDE, C), F32),
            pltpu.VMEM((C, C), F32),
            pltpu.VMEM((nrows, C), F32),
            pltpu.VMEM((ncols, C), F32),
            pltpu.VMEM((144, C), F32),
        ],
        compiler_params=pltpu.CompilerParams(vmem_limit_bytes=16 * 1024 * 1024),
        name="finish",
    )(own, other, wr, wc, w)


def swap(a):
    return lax.ppermute(a, "c", [(0, 1), (1, 0)])


def shards(cot, prev, single_rows, single_cols, w_row, w_col, w_rec, gain, bias, ids_rows, ids_cols):
    nrows, ncols = cot.shape[:2]
    gain2, bias2 = gain.reshape(1, C), bias.reshape(1, C)
    send, keep, col_part, d_prev = local_reductions(
        cot, prev, w_rec, gain2, bias2, ids_rows, ids_cols, single_rows, single_cols
    )
    (shares,) = glue(plane_kernel, "plane", [(PLANE, WIDE)], keep, swap(send), col_part)
    got = lax.all_to_all(shares, XY, 0, 0)
    shares, mine = glue(line_kernel, "line", [(LINE, SHARED + 4 * COLS_AT), (4 * COLS_AT,)], got)
    got = lax.all_to_all(shares, Z, 0, 0)
    (shares,) = glue(spread_kernel, "spread", [(PLANE, WIDE)], got, mine)
    own = lax.all_to_all(shares, XY, 0, 0)
    dsr, dsc, dwr, dwc, rec, rel, dg, db = finish(own, swap(own), w_row, w_col, w_rec, nrows, ncols)
    return d_prev, dsr, dsc, dwr, dwc, rec, rel, dg.reshape(C), db.reshape(C)


def solution(mesh):
    fine = Mesh(mesh.devices.reshape(2, 4, 4, 4, 2), ("zh", "x", "y", "zl", "c"))
    return jax.shard_map(
        shards,
        mesh=fine,
        in_specs=(
            P(ROW, COL, None), P(ROW, COL, None), P(ROW, None), P(COL, None),
            P(), P(), P(), P(), P(), P(None, ROW), P(None, COL),
        ),
        out_specs=(P(ROW, COL, None), P(ROW, None), P(COL, None), P(), P(), P(), P(), P(), P()),
        check_vma=False,
    )
```

```python
import functools

import jax
import jax.numpy as jnp
from jax import lax
from jax.experimental import pallas as pl
from jax.experimental.pallas import tpu as pltpu
from jax.sharding import Mesh, PartitionSpec as P

F32, BF16 = jnp.float32, jnp.bfloat16
C = 128
S = 384
BINS = 139
SUB = 16
SHARED = 33
ROWS_AT, COLS_AT = 4, 7
CHUNK = SHARED + ROWS_AT
WIDE = CHUNK + COLS_AT
PARTS = 32
PLANE, LINE = 16, 8
VMEM = 40 * 1024 * 1024
XY, Z = ("x", "y"), ("zh", "zl")
ROW, COL = ("zh", "x"), ("y", "zl", "c")


def dot(a, b, dims):
    return lax.dot_general(a, b, (dims, ((), ())), preferred_element_type=F32)


def split_dot(a, b, dims, split_left):
    x = a if split_left else b
    hi = x.astype(BF16)
    low = (x - hi.astype(F32)).astype(BF16)
    if split_left:
        return dot(hi, b, dims) + dot(low, b, dims)
    return dot(a, hi, dims) + dot(a, low, dims)


def reduce_kernel(cols, rows, cot_hbm, prev_hbm, w_hbm, gain_hbm, bias_hbm, idr_hbm, idc_hbm, sr_hbm, sc_hbm,
                  send_ref, keep_ref, colp_ref, dprev_hbm,
                  cot_ref, prev_ref, dprev_ref, w_ref, gain_ref, bias_ref, idr_ref, idc_ref, sr_ref, sc_ref,
                  acc, gains, gcol, bcol, rowp, buf, small_sems, in_sems, out_sems):
    units = rows // SUB
    small = [
        pltpu.make_async_copy(src, dst, small_sems.at[k])
        for k, (src, dst) in enumerate((
            (gain_hbm, gain_ref), (bias_hbm, bias_ref), (w_hbm, w_ref), (idr_hbm, idr_ref), (idc_hbm, idc_ref),
            (sr_hbm, sr_ref), (sc_hbm, sc_ref),
        ))
    ]

    def part(u):
        return pl.ds(pl.multiple_of(u * SUB, SUB), SUB)

    def fetch(u):
        return [
            pltpu.make_async_copy(src.at[part(u)], dst.at[part(u)], in_sems.at[k, u])
            for k, (src, dst) in enumerate(((prev_hbm, prev_ref), (cot_hbm, cot_ref)))
        ]

    def put(u):
        return pltpu.make_async_copy(dprev_ref.at[part(u)], dprev_hbm.at[part(u)], out_sems.at[u])

    for copy in small[:5] + fetch(0) + fetch(1) + small[5:]:
        copy.start()
    acc[...] = jnp.zeros_like(acc)
    gains[...] = jnp.zeros_like(gains)
    colp_ref[...] = jnp.zeros_like(colp_ref)
    for copy in small[:5]:
        copy.wait()
    gcol[...] = jnp.transpose(jnp.broadcast_to(gain_ref[...], (C, C)))
    bcol[...] = jnp.transpose(jnp.broadcast_to(bias_ref[...], (C, C)))

    n = SUB * cols
    idr = idr_ref[...].astype(F32)
    idc = idc_ref[...].astype(F32)
    gain, bias = gcol[:, 0:1], bcol[:, 0:1]
    lane = lax.broadcasted_iota(jnp.int32, (SUB, idr.shape[1]), 1)
    sub = lax.broadcasted_iota(jnp.int32, (SUB, idr.shape[1]), 0)
    flat_lane = lax.broadcasted_iota(jnp.int32, (16, n), 1)
    flat_sub = lax.broadcasted_iota(jnp.int32, (16, n), 0)
    rowind = jnp.where((flat_lane >= flat_sub * cols) & (flat_lane < (flat_sub + 1) * cols), 1.0, 0.0).astype(BF16)

    eye = lax.broadcasted_iota(jnp.int32, (C, C), 0) == lax.broadcasted_iota(jnp.int32, (C, C), 1)
    centering = (jnp.where(eye, 1.0, 0.0) - 1.0 / C).astype(BF16)

    w = w_ref[...]
    lead = jnp.sum(w.astype(F32) * gcol[...], axis=0, keepdims=True) * (1.0 / C)
    lead_hi = lead.astype(BF16).astype(F32)
    sub16 = lax.broadcasted_iota(jnp.int32, (16, C), 0)
    extra = jnp.where(sub16 == 0, lead_hi, jnp.where(sub16 == 1, lead - lead_hi, 0.0))
    wide_w = jnp.concatenate([w, extra.astype(BF16)], axis=0)

    def mean(a):
        return jnp.sum(a, axis=0, keepdims=True) * (1.0 / C)

    def unit(u):
        first = u * SUB
        here = part(u)
        cot = cot_ref[here].reshape(n, C)
        centered = dot(centering, prev_ref[here].reshape(n, C), ((1,), (1,)))
        rstd = lax.rsqrt(mean(centered * centered) + 1e-05)
        xhat = centered * rstd
        normed = (xhat * gain + bias).astype(BF16)
        y = dot(wide_w, cot, ((1,), (1,)))
        g = y[:C] * gain
        g_mean = y[C:C + 1] + y[C + 1:C + 2]
        gx = g * xhat
        share = gx[:, 0:C]
        for lo in range(C, n, C):
            share += gx[:, lo:lo + C]
        gains[...] += share
        res = (rstd * (g - g_mean - xhat * mean(gx))).astype(BF16)
        dprev_ref[here] = jnp.transpose(res).reshape(SUB, cols, C)
        mask = lane == sub + first
        di = [jnp.sum(jnp.where(mask, idr[k:k + 1], 0.0), axis=1, keepdims=True) for k in range(5)]
        dj = [idc[k:k + 1] for k in range(5)]
        same_chain = di[2] == dj[2]
        same_res = same_chain & (di[0] == dj[0])
        same_entity = di[3] == dj[3]
        r = jnp.where(same_chain, jnp.clip(di[0] - dj[0] + 32.0, 0.0, 64.0), 65.0)
        t = jnp.where(same_res, jnp.clip(di[1] - dj[1] + 32.0, 0.0, 64.0), 65.0)
        c = jnp.where(same_entity & jnp.logical_not(same_chain), jnp.clip(di[4] - dj[4] + 2.0, 0.0, 4.0), 5.0)
        packed = (r + 128.0 * t + 16384.0 * c).astype(jnp.int32) + jnp.where(same_entity, 1 << 18, 0)
        packed = jnp.concatenate([packed[s:s + 1] for s in range(SUB)], axis=1)
        r, t, c = packed & 127, ((packed >> 7) & 127) + 66, ((packed >> 14) & 15) + 133
        e = jnp.where(packed >= 1 << 18, 132, -1)

        def hot(lo, hi, *codes):
            q = (lax.broadcasted_iota(jnp.int32, (hi - lo, n), 0) + lo).astype(BF16)
            codes = [code.astype(BF16) for code in codes]
            hit = q == codes[0]
            for code in codes[1:]:
                hit = hit | (q == code)
            return jnp.where(hit, jnp.ones((), BF16), jnp.zeros((), BF16))

        left = jnp.concatenate(
            [normed, hot(0, 64, r), hot(64, 80, r, t), hot(80, 128, t), hot(128, 144, t, e, c), rowind], axis=0
        )
        out = dot(left, cot, ((1,), (0,)))
        acc[...] += out[:272]
        rowp[here, :] = out[272:288]
        wide = cot[:cols].astype(F32)
        for s in range(1, SUB):
            wide += cot[s * cols:(s + 1) * cols].astype(F32)
        colp_ref[...] += wide

    @pl.loop(0, units // 2, unroll=1)
    def _(v):
        for j in range(2):
            for copy in fetch(v * 2 + j):
                copy.wait()

        @pl.when(v + 1 < units // 2)
        def _():
            for j in range(2):
                for copy in fetch((v + 1) * 2 + j):
                    copy.start()

        for j in range(2):
            unit(v * 2 + j)
        for j in range(2):
            put(v * 2 + j).start()

    for copy in small[5:]:
        copy.wait()
    dwr = split_dot(sr_ref[...], rowp[...], ((0,), (0,)), False)
    dwc = split_dot(sc_ref[...], colp_ref[...], ((0,), (0,)), False)
    acc[267:268] = jnp.sum(jnp.transpose(gains[...]), axis=0, keepdims=True) / gain_ref[...]
    total = acc[...]
    for k in range(PARTS):
        half, at = k // PLANE, k % PLANE * CHUNK
        buf[half, at:at + 12] = dwr[12 * k:12 * k + 12]
        buf[half, at + 12:at + 24] = dwc[12 * k:12 * k + 12]
        buf[half, at + 24:at + 28] = total[4 * k:4 * k + 4]
        lo, hi = 128 + 5 * k, min(128 + 5 * k + 5, 272)
        if lo < hi:
            buf[half, at + 28:at + 28 + hi - lo] = total[lo:hi]
        if hi - lo < 5:
            buf[half, at + 28 + max(hi - lo, 0):at + SHARED] = jnp.zeros((5 - max(hi - lo, 0), C), F32)
        buf[half, at + SHARED:at + CHUNK] = rowp[ROWS_AT * k:ROWS_AT * (k + 1)]
    core = lax.axis_index("c")
    keep_ref[...] = buf[core]
    send_ref[...] = buf[1 - core]

    @pl.loop(0, units)
    def _(u):
        put(u).wait()


def local_reductions(cot, prev, w, gain, bias, idr, idc, sr, sc):
    rows, cols = cot.shape[:2]
    units = rows // SUB
    part = jax.ShapeDtypeStruct((PLANE * CHUNK, C), F32)
    hbm, vmem = pl.BlockSpec(memory_space=pltpu.HBM), pl.BlockSpec(memory_space=pltpu.VMEM)
    same = lambda a: pltpu.VMEM(a.shape, a.dtype)
    arrays = (cot, prev, w, gain, bias, idr, idc, sr, sc)
    return pl.pallas_call(
        functools.partial(reduce_kernel, cols, rows),
        in_specs=[hbm] * 9,
        out_specs=[vmem, vmem, vmem, hbm],
        out_shape=[part, part, jax.ShapeDtypeStruct((cols, C), F32), jax.ShapeDtypeStruct(cot.shape, BF16)],
        scratch_shapes=[same(cot), same(prev), same(cot)] + [same(a) for a in arrays[2:]] + [
            pltpu.VMEM((272, C), F32),
            pltpu.VMEM((C, C), F32),
            pltpu.VMEM((C, C), F32),
            pltpu.VMEM((C, C), F32),
            pltpu.VMEM((rows, C), F32),
            pltpu.VMEM((2,) + part.shape, F32),
            pltpu.SemaphoreType.DMA((7,)),
            pltpu.SemaphoreType.DMA((2, units)),
            pltpu.SemaphoreType.DMA((units,)),
        ],
        compiler_params=pltpu.CompilerParams(vmem_limit_bytes=VMEM),
        name="local_reductions",
    )(*[pltpu.with_memory_space_constraint(a, pltpu.HBM) for a in arrays])


def plane_kernel(keep_ref, got_ref, colp_ref, out_ref):
    for k in range(PLANE):
        at = slice(CHUNK * k, CHUNK * (k + 1))
        out_ref[k, 0:CHUNK] = keep_ref[at] + got_ref[at]
        out_ref[k, CHUNK:] = colp_ref[COLS_AT * k:COLS_AT * (k + 1)]


def line_kernel(r_ref, out_ref, mine_ref):
    zh, zl = lax.axis_index("zh"), lax.axis_index("zl")
    total = r_ref[0, 0:SHARED]
    for k in range(1, PLANE):
        total += r_ref[k, 0:SHARED]
    for i in range(4):
        part = r_ref[i, CHUNK:]
        for j in range(1, 4):
            part += r_ref[4 * j + i, CHUNK:]
        mine_ref[COLS_AT * i:COLS_AT * (i + 1)] = part
    for k in range(LINE):
        out_ref[k, 0:SHARED] = total
        out_ref[k, SHARED:] = jnp.zeros((4 * COLS_AT, C), F32)
    for i in range(4):
        part = r_ref[4 * i, SHARED:CHUNK]
        for j in range(1, 4):
            part += r_ref[4 * i + j, SHARED:CHUNK]
        at = SHARED + ROWS_AT * i
        for j in range(4):
            out_ref[4 * zh + j, at:at + ROWS_AT] = part
    out_ref[4 * (1 - zh) + zl, SHARED:] = mine_ref[...]


def spread_kernel(r_ref, mine_ref, out_ref):
    zh, zl = lax.axis_index("zh"), lax.axis_index("zl")
    total = r_ref[0, 0:SHARED]
    for k in range(1, LINE):
        total += r_ref[k, 0:SHARED]
    rows = r_ref[4 * zh, SHARED:SHARED + 4 * ROWS_AT]
    for j in range(1, 4):
        rows += r_ref[4 * zh + j, SHARED:SHARED + 4 * ROWS_AT]
    cols = mine_ref[...] + r_ref[4 * (1 - zh) + zl, SHARED:]
    for k in range(PLANE):
        i, j = k // 4, k % 4
        out_ref[k, 0:SHARED] = total
        out_ref[k, SHARED:CHUNK] = rows[ROWS_AT * i:ROWS_AT * (i + 1)]
        out_ref[k, CHUNK:] = cols[COLS_AT * j:COLS_AT * (j + 1)]


def glue(kernel, name, outs, *args):
    vmem = pl.BlockSpec(memory_space=pltpu.VMEM)
    return pl.pallas_call(
        kernel,
        in_specs=[vmem] * len(args),
        out_specs=[vmem] * len(outs),
        out_shape=[jax.ShapeDtypeStruct(shape + (C,), F32) for shape in outs],
        compiler_params=pltpu.CompilerParams(vmem_limit_bytes=16 * 1024 * 1024),
        name=name,
    )(*args)


def final_kernel(own_ref, other_ref, wr_ref, wc_ref, w_ref,
                 dsr_ref, dsc_ref, dwr_ref, dwc_ref, rec_ref, rel_ref, dg_ref, db_ref, buf, m, rows, cols, rel):
    core = lax.axis_index("c")
    buf[core] = own_ref[...]
    buf[1 - core] = other_ref[...]
    for k in range(PARTS):
        half, place = k // PLANE, k % PLANE
        dwr_ref[12 * k:12 * k + 12] = buf[half, place, 0:12]
        dwc_ref[12 * k:12 * k + 12] = buf[half, place, 12:24]
        m[4 * k:4 * k + 4] = buf[half, place, 24:28]
        lo, hi = 5 * k, min(5 * k + 5, 144)
        if lo < hi:
            rel[lo:hi] = buf[half, place, 28:28 + hi - lo]
        rows[ROWS_AT * k:ROWS_AT * (k + 1)] = buf[half, place, SHARED:CHUNK]
    for k in range(PLANE):
        cols[COLS_AT * k:COLS_AT * (k + 1)] = own_ref[k, CHUNK:]
    rel_ref[...] = rel[0:BINS]
    total = jnp.sum(rel[133:139], axis=0, keepdims=True)
    w = w_ref[...].astype(F32)
    rec_ref[...] = m[...]
    dg_ref[...] = rel[BINS:BINS + 1]
    db_ref[...] = jnp.sum(jnp.transpose(w * total), axis=0, keepdims=True)
    dsr_ref[...] = split_dot(rows[...], wr_ref[...], ((1,), (1,)), True)
    dsc_ref[...] = split_dot(cols[...], wc_ref[...], ((1,), (1,)), True)


def finish(own, other, wr, wc, w, nrows, ncols):
    f = lambda *s: jax.ShapeDtypeStruct(s, F32)
    vmem = pl.BlockSpec(memory_space=pltpu.VMEM)
    return pl.pallas_call(
        final_kernel,
        in_specs=[vmem] * 5,
        out_specs=[vmem] * 8,
        out_shape=[f(nrows, S), f(ncols, S), f(S, C), f(S, C), f(C, C), f(BINS, C), f(1, C), f(1, C)],
        scratch_shapes=[
            pltpu.VMEM((2, PLANE, WIDE, C), F32),
            pltpu.VMEM((C, C), F32),
            pltpu.VMEM((nrows, C), F32),
            pltpu.VMEM((ncols, C), F32),
            pltpu.VMEM((144, C), F32),
        ],
        compiler_params=pltpu.CompilerParams(vmem_limit_bytes=16 * 1024 * 1024),
        name="finish",
    )(own, other, wr, wc, w)


def swap(a):
    return lax.ppermute(a, "c", [(0, 1), (1, 0)])


def shards(cot, prev, single_rows, single_cols, w_row, w_col, w_rec, gain, bias, ids_rows, ids_cols):
    nrows, ncols = cot.shape[:2]
    gain2, bias2 = gain.reshape(1, C), bias.reshape(1, C)
    send, keep, col_part, d_prev = local_reductions(
        cot, prev, w_rec, gain2, bias2, ids_rows, ids_cols, single_rows, single_cols
    )
    (shares,) = glue(plane_kernel, "plane", [(PLANE, WIDE)], keep, swap(send), col_part)
    got = lax.all_to_all(shares, XY, 0, 0)
    shares, mine = glue(line_kernel, "line", [(LINE, SHARED + 4 * COLS_AT), (4 * COLS_AT,)], got)
    got = lax.all_to_all(shares, Z, 0, 0)
    (shares,) = glue(spread_kernel, "spread", [(PLANE, WIDE)], got, mine)
    own = lax.all_to_all(shares, XY, 0, 0)
    dsr, dsc, dwr, dwc, rec, rel, dg, db = finish(own, swap(own), w_row, w_col, w_rec, nrows, ncols)
    return d_prev, dsr, dsc, dwr, dwc, rec, rel, dg.reshape(C), db.reshape(C)


def solution(mesh):
    fine = Mesh(mesh.devices.reshape(2, 4, 4, 4, 2), ("zh", "x", "y", "zl", "c"))
    return jax.shard_map(
        shards,
        mesh=fine,
        in_specs=(
            P(ROW, COL, None), P(ROW, COL, None), P(ROW, None), P(COL, None),
            P(), P(), P(), P(), P(), P(None, ROW), P(None, COL),
        ),
        out_specs=(P(ROW, COL, None), P(ROW, None), P(COL, None), P(), P(), P(), P(), P(), P()),
        check_vma=False,
    )
```

```python
import functools

import jax
import jax.numpy as jnp
from jax import lax
from jax.experimental import pallas as pl
from jax.experimental.pallas import tpu as pltpu
from jax.sharding import Mesh, PartitionSpec as P

F32, BF16 = jnp.float32, jnp.bfloat16
C = 128
S = 384
BINS = 139
SUB = 16
SHARED = 33
ROWS_AT, COLS_AT = 4, 7
CHUNK = SHARED + ROWS_AT
WIDE = CHUNK + COLS_AT
PARTS = 32
PLANE, LINE = 16, 8
VMEM = 40 * 1024 * 1024
XY, Z = ("x", "y"), ("zl", "zh")
ROW, COL = ("zh", "x"), ("y", "zl", "c")


def dot(a, b, dims):
    return lax.dot_general(a, b, (dims, ((), ())), preferred_element_type=F32)


def split_dot(a, b, dims, split_left):
    x = a if split_left else b
    hi = x.astype(BF16)
    low = (x - hi.astype(F32)).astype(BF16)
    if split_left:
        return dot(hi, b, dims) + dot(low, b, dims)
    return dot(a, hi, dims) + dot(a, low, dims)


def reduce_kernel(cols, rows, cot_hbm, prev_hbm, w_hbm, gain_hbm, bias_hbm, idr_hbm, idc_hbm, sr_hbm, sc_hbm,
                  send_ref, keep_ref, colp_ref, dprev_hbm,
                  cot_ref, prev_ref, dprev_ref, w_ref, gain_ref, bias_ref, idr_ref, idc_ref, sr_ref, sc_ref,
                  acc, gains, gcol, bcol, rowp, buf, small_sems, in_sems, out_sems):
    units = rows // SUB
    small = [
        pltpu.make_async_copy(src, dst, small_sems.at[k])
        for k, (src, dst) in enumerate((
            (gain_hbm, gain_ref), (bias_hbm, bias_ref), (w_hbm, w_ref), (idr_hbm, idr_ref), (idc_hbm, idc_ref),
            (sr_hbm, sr_ref), (sc_hbm, sc_ref),
        ))
    ]

    def part(u):
        return pl.ds(pl.multiple_of(u * SUB, SUB), SUB)

    def fetch(u):
        return [
            pltpu.make_async_copy(src.at[part(u)], dst.at[part(u)], in_sems.at[k, u])
            for k, (src, dst) in enumerate(((prev_hbm, prev_ref), (cot_hbm, cot_ref)))
        ]

    def put(u):
        return pltpu.make_async_copy(dprev_ref.at[part(u)], dprev_hbm.at[part(u)], out_sems.at[u])

    for copy in small[:5] + fetch(0) + fetch(1) + small[5:]:
        copy.start()
    acc[...] = jnp.zeros_like(acc)
    gains[...] = jnp.zeros_like(gains)
    colp_ref[...] = jnp.zeros_like(colp_ref)
    for copy in small[:5]:
        copy.wait()
    gcol[...] = jnp.transpose(jnp.broadcast_to(gain_ref[...], (C, C)))
    bcol[...] = jnp.transpose(jnp.broadcast_to(bias_ref[...], (C, C)))

    n = SUB * cols
    idr = idr_ref[...].astype(F32)
    idc = idc_ref[...].astype(F32)
    gain, bias = gcol[:, 0:1], bcol[:, 0:1]
    lane = lax.broadcasted_iota(jnp.int32, (SUB, idr.shape[1]), 1)
    sub = lax.broadcasted_iota(jnp.int32, (SUB, idr.shape[1]), 0)
    flat_lane = lax.broadcasted_iota(jnp.int32, (16, n), 1)
    flat_sub = lax.broadcasted_iota(jnp.int32, (16, n), 0)
    rowind = jnp.where((flat_lane >= flat_sub * cols) & (flat_lane < (flat_sub + 1) * cols), 1.0, 0.0).astype(BF16)

    eye = lax.broadcasted_iota(jnp.int32, (C, C), 0) == lax.broadcasted_iota(jnp.int32, (C, C), 1)
    centering = (jnp.where(eye, 1.0, 0.0) - 1.0 / C).astype(BF16)

    w = w_ref[...]
    lead = jnp.sum(w.astype(F32) * gcol[...], axis=0, keepdims=True) * (1.0 / C)
    lead_hi = lead.astype(BF16).astype(F32)
    sub16 = lax.broadcasted_iota(jnp.int32, (16, C), 0)
    extra = jnp.where(sub16 == 0, lead_hi, jnp.where(sub16 == 1, lead - lead_hi, 0.0))
    wide_w = jnp.concatenate([w, extra.astype(BF16)], axis=0)

    def mean(a):
        return jnp.sum(a, axis=0, keepdims=True) * (1.0 / C)

    def unit(u):
        first = u * SUB
        here = part(u)
        cot = cot_ref[here].reshape(n, C)
        centered = dot(centering, prev_ref[here].reshape(n, C), ((1,), (1,)))
        rstd = lax.rsqrt(mean(centered * centered) + 1e-05)
        xhat = centered * rstd
        normed = (xhat * gain + bias).astype(BF16)
        y = dot(wide_w, cot, ((1,), (1,)))
        g = y[:C] * gain
        g_mean = y[C:C + 1] + y[C + 1:C + 2]
        gx = g * xhat
        share = gx[:, 0:C]
        for lo in range(C, n, C):
            share += gx[:, lo:lo + C]
        gains[...] += share
        res = (rstd * (g - g_mean - xhat * mean(gx))).astype(BF16)
        dprev_ref[here] = jnp.transpose(res).reshape(SUB, cols, C)
        mask = lane == sub + first
        di = [jnp.sum(jnp.where(mask, idr[k:k + 1], 0.0), axis=1, keepdims=True) for k in range(5)]
        dj = [idc[k:k + 1] for k in range(5)]
        same_chain = di[2] == dj[2]
        same_res = same_chain & (di[0] == dj[0])
        same_entity = di[3] == dj[3]
        r = jnp.where(same_chain, jnp.clip(di[0] - dj[0] + 32.0, 0.0, 64.0), 65.0)
        t = jnp.where(same_res, jnp.clip(di[1] - dj[1] + 32.0, 0.0, 64.0), 65.0)
        c = jnp.where(same_entity & jnp.logical_not(same_chain), jnp.clip(di[4] - dj[4] + 2.0, 0.0, 4.0), 5.0)
        packed = (r + 128.0 * t + 16384.0 * c).astype(jnp.int32) + jnp.where(same_entity, 1 << 18, 0)
        packed = jnp.concatenate([packed[s:s + 1] for s in range(SUB)], axis=1)
        r, t, c = packed & 127, ((packed >> 7) & 127) + 66, ((packed >> 14) & 15) + 133
        e = jnp.where(packed >= 1 << 18, 132, -1)

        def hot(lo, hi, *codes):
            q = (lax.broadcasted_iota(jnp.int32, (hi - lo, n), 0) + lo).astype(BF16)
            codes = [code.astype(BF16) for code in codes]
            hit = q == codes[0]
            for code in codes[1:]:
                hit = hit | (q == code)
            return jnp.where(hit, jnp.ones((), BF16), jnp.zeros((), BF16))

        left = jnp.concatenate(
            [normed, hot(0, 64, r), hot(64, 80, r, t), hot(80, 128, t), hot(128, 144, t, e, c), rowind], axis=0
        )
        out = dot(left, cot, ((1,), (0,)))
        acc[...] += out[:272]
        rowp[here, :] = out[272:288]
        wide = cot[:cols].astype(F32)
        for s in range(1, SUB):
            wide += cot[s * cols:(s + 1) * cols].astype(F32)
        colp_ref[...] += wide

    @pl.loop(0, units // 2, unroll=1)
    def _(v):
        for j in range(2):
            for copy in fetch(v * 2 + j):
                copy.wait()

        @pl.when(v + 1 < units // 2)
        def _():
            for j in range(2):
                for copy in fetch((v + 1) * 2 + j):
                    copy.start()

        for j in range(2):
            unit(v * 2 + j)
        for j in range(2):
            put(v * 2 + j).start()

    for copy in small[5:]:
        copy.wait()
    dwr = split_dot(sr_ref[...], rowp[...], ((0,), (0,)), False)
    dwc = split_dot(sc_ref[...], colp_ref[...], ((0,), (0,)), False)
    acc[267:268] = jnp.sum(jnp.transpose(gains[...]), axis=0, keepdims=True) / gain_ref[...]
    total = acc[...]
    for k in range(PARTS):
        half, at = k // PLANE, k % PLANE * CHUNK
        buf[half, at:at + 12] = dwr[12 * k:12 * k + 12]
        buf[half, at + 12:at + 24] = dwc[12 * k:12 * k + 12]
        buf[half, at + 24:at + 28] = total[4 * k:4 * k + 4]
        lo, hi = 128 + 5 * k, min(128 + 5 * k + 5, 272)
        if lo < hi:
            buf[half, at + 28:at + 28 + hi - lo] = total[lo:hi]
        if hi - lo < 5:
            buf[half, at + 28 + max(hi - lo, 0):at + SHARED] = jnp.zeros((5 - max(hi - lo, 0), C), F32)
        buf[half, at + SHARED:at + CHUNK] = rowp[ROWS_AT * k:ROWS_AT * (k + 1)]
    core = lax.axis_index("c")
    keep_ref[...] = buf[core]
    send_ref[...] = buf[1 - core]

    @pl.loop(0, units)
    def _(u):
        put(u).wait()


def local_reductions(cot, prev, w, gain, bias, idr, idc, sr, sc):
    rows, cols = cot.shape[:2]
    units = rows // SUB
    part = jax.ShapeDtypeStruct((PLANE * CHUNK, C), F32)
    hbm, vmem = pl.BlockSpec(memory_space=pltpu.HBM), pl.BlockSpec(memory_space=pltpu.VMEM)
    same = lambda a: pltpu.VMEM(a.shape, a.dtype)
    arrays = (cot, prev, w, gain, bias, idr, idc, sr, sc)
    return pl.pallas_call(
        functools.partial(reduce_kernel, cols, rows),
        in_specs=[hbm] * 9,
        out_specs=[vmem, vmem, vmem, hbm],
        out_shape=[part, part, jax.ShapeDtypeStruct((cols, C), F32), jax.ShapeDtypeStruct(cot.shape, BF16)],
        scratch_shapes=[same(cot), same(prev), same(cot)] + [same(a) for a in arrays[2:]] + [
            pltpu.VMEM((272, C), F32),
            pltpu.VMEM((C, C), F32),
            pltpu.VMEM((C, C), F32),
            pltpu.VMEM((C, C), F32),
            pltpu.VMEM((rows, C), F32),
            pltpu.VMEM((2,) + part.shape, F32),
            pltpu.SemaphoreType.DMA((7,)),
            pltpu.SemaphoreType.DMA((2, units)),
            pltpu.SemaphoreType.DMA((units,)),
        ],
        compiler_params=pltpu.CompilerParams(vmem_limit_bytes=VMEM),
        name="local_reductions",
    )(*[pltpu.with_memory_space_constraint(a, pltpu.HBM) for a in arrays])


def plane_kernel(keep_ref, got_ref, colp_ref, out_ref):
    for k in range(PLANE):
        at = slice(CHUNK * k, CHUNK * (k + 1))
        out_ref[k, 0:CHUNK] = keep_ref[at] + got_ref[at]
        out_ref[k, CHUNK:] = colp_ref[COLS_AT * k:COLS_AT * (k + 1)]


def line_kernel(r_ref, out_ref, mine_ref):
    zh, zl = lax.axis_index("zh"), lax.axis_index("zl")
    total = r_ref[0, 0:SHARED]
    for k in range(1, PLANE):
        total += r_ref[k, 0:SHARED]
    for i in range(4):
        part = r_ref[i, CHUNK:]
        for j in range(1, 4):
            part += r_ref[4 * j + i, CHUNK:]
        mine_ref[COLS_AT * i:COLS_AT * (i + 1)] = part
    for k in range(LINE):
        out_ref[k, 0:SHARED] = total
        out_ref[k, SHARED:] = jnp.zeros((4 * COLS_AT, C), F32)
    for i in range(4):
        part = r_ref[4 * i, SHARED:CHUNK]
        for j in range(1, 4):
            part += r_ref[4 * i + j, SHARED:CHUNK]
        at = SHARED + ROWS_AT * i
        for j in range(4):
            out_ref[2 * j + zh, at:at + ROWS_AT] = part
    out_ref[2 * zl + 1 - zh, SHARED:] = mine_ref[...]


def spread_kernel(r_ref, mine_ref, out_ref):
    zh, zl = lax.axis_index("zh"), lax.axis_index("zl")
    total = r_ref[0, 0:SHARED]
    for k in range(1, LINE):
        total += r_ref[k, 0:SHARED]
    rows = r_ref[zh, SHARED:SHARED + 4 * ROWS_AT]
    for j in range(1, 4):
        rows += r_ref[2 * j + zh, SHARED:SHARED + 4 * ROWS_AT]
    cols = mine_ref[...] + r_ref[2 * zl + 1 - zh, SHARED:]
    for k in range(PLANE):
        i, j = k // 4, k % 4
        out_ref[k, 0:SHARED] = total
        out_ref[k, SHARED:CHUNK] = rows[ROWS_AT * i:ROWS_AT * (i + 1)]
        out_ref[k, CHUNK:] = cols[COLS_AT * j:COLS_AT * (j + 1)]


def glue(kernel, name, outs, *args):
    vmem = pl.BlockSpec(memory_space=pltpu.VMEM)
    return pl.pallas_call(
        kernel,
        in_specs=[vmem] * len(args),
        out_specs=[vmem] * len(outs),
        out_shape=[jax.ShapeDtypeStruct(shape + (C,), F32) for shape in outs],
        compiler_params=pltpu.CompilerParams(vmem_limit_bytes=16 * 1024 * 1024),
        name=name,
    )(*args)


def cols_kernel(own_ref, wc_ref, dsc_ref, cols):
    for k in range(PLANE):
        cols[COLS_AT * k:COLS_AT * (k + 1)] = own_ref[k, CHUNK:]
    dsc_ref[...] = split_dot(cols[...], wc_ref[...], ((1,), (1,)), True)


def finish_cols(own, wc, ncols):
    vmem = pl.BlockSpec(memory_space=pltpu.VMEM)
    return pl.pallas_call(
        cols_kernel,
        in_specs=[vmem] * 2,
        out_specs=vmem,
        out_shape=jax.ShapeDtypeStruct((ncols, S), F32),
        scratch_shapes=[pltpu.VMEM((ncols, C), F32)],
        compiler_params=pltpu.CompilerParams(vmem_limit_bytes=16 * 1024 * 1024),
        name="finish_cols",
    )(own, wc)


def final_kernel(own_ref, other_ref, wr_ref, w_ref,
                 dsr_ref, dwr_ref, dwc_ref, rec_ref, rel_ref, dg_ref, db_ref, buf, m, rows, rel):
    core = lax.axis_index("c")
    buf[core] = own_ref[...]
    buf[1 - core] = other_ref[...]
    for k in range(PARTS):
        half, place = k // PLANE, k % PLANE
        dwr_ref[12 * k:12 * k + 12] = buf[half, place, 0:12]
        dwc_ref[12 * k:12 * k + 12] = buf[half, place, 12:24]
        m[4 * k:4 * k + 4] = buf[half, place, 24:28]
        lo, hi = 5 * k, min(5 * k + 5, 144)
        if lo < hi:
            rel[lo:hi] = buf[half, place, 28:28 + hi - lo]
        rows[ROWS_AT * k:ROWS_AT * (k + 1)] = buf[half, place, SHARED:CHUNK]
    rel_ref[...] = rel[0:BINS]
    total = jnp.sum(rel[133:139], axis=0, keepdims=True)
    w = w_ref[...].astype(F32)
    rec_ref[...] = m[...]
    dg_ref[...] = rel[BINS:BINS + 1]
    db_ref[...] = jnp.sum(jnp.transpose(w * total), axis=0, keepdims=True)
    dsr_ref[...] = split_dot(rows[...], wr_ref[...], ((1,), (1,)), True)


def finish(own, other, wr, w, nrows):
    f = lambda *s: jax.ShapeDtypeStruct(s, F32)
    vmem = pl.BlockSpec(memory_space=pltpu.VMEM)
    return pl.pallas_call(
        final_kernel,
        in_specs=[vmem] * 4,
        out_specs=[vmem] * 7,
        out_shape=[f(nrows, S), f(S, C), f(S, C), f(C, C), f(BINS, C), f(1, C), f(1, C)],
        scratch_shapes=[
            pltpu.VMEM((2, PLANE, WIDE, C), F32),
            pltpu.VMEM((C, C), F32),
            pltpu.VMEM((nrows, C), F32),
            pltpu.VMEM((144, C), F32),
        ],
        compiler_params=pltpu.CompilerParams(vmem_limit_bytes=16 * 1024 * 1024),
        name="finish",
    )(own, other, wr, w)


def swap(a):
    return lax.ppermute(a, "c", [(0, 1), (1, 0)])


def shards(cot, prev, single_rows, single_cols, w_row, w_col, w_rec, gain, bias, ids_rows, ids_cols):
    nrows, ncols = cot.shape[:2]
    gain2, bias2 = gain.reshape(1, C), bias.reshape(1, C)
    send, keep, col_part, d_prev = local_reductions(
        cot, prev, w_rec, gain2, bias2, ids_rows, ids_cols, single_rows, single_cols
    )
    (shares,) = glue(plane_kernel, "plane", [(PLANE, WIDE)], keep, swap(send), col_part)
    got = lax.all_to_all(shares, XY, 0, 0)
    shares, mine = glue(line_kernel, "line", [(LINE, SHARED + 4 * COLS_AT), (4 * COLS_AT,)], got)
    got = lax.all_to_all(shares, Z, 0, 0)
    (shares,) = glue(spread_kernel, "spread", [(PLANE, WIDE)], got, mine)
    own = lax.all_to_all(shares, XY, 0, 0)
    dsc = finish_cols(own, w_col, ncols)
    dsr, dwr, dwc, rec, rel, dg, db = finish(own, swap(own), w_row, w_rec, nrows)
    return d_prev, dsr, dsc, dwr, dwc, rec, rel, dg.reshape(C), db.reshape(C)


def solution(mesh):
    fine = Mesh(mesh.devices.reshape(2, 4, 4, 4, 2), ("zh", "x", "y", "zl", "c"))
    return jax.shard_map(
        shards,
        mesh=fine,
        in_specs=(
            P(ROW, COL, None), P(ROW, COL, None), P(ROW, None), P(COL, None),
            P(), P(), P(), P(), P(), P(None, ROW), P(None, COL),
        ),
        out_specs=(P(ROW, COL, None), P(ROW, None), P(COL, None), P(), P(), P(), P(), P(), P()),
        check_vma=False,
    )
```
